32 devices in a mesh: dp: 4 (over z), expert: 8 (over y, x, core).
Axes of the slice: x: 2, y: 2, z: 4, core: 2. Of those that a mesh axis runs over, the one named last changes fastest.
Arguments:
- cotangent: bfloat16 [4096, 1440], P(('dp', 'expert')), may hold values from -0.0625 to 0.0625
- gates: bfloat16 [4096, 4], P(('dp', 'expert')), may hold values from 0.049804688 to 0.59765625
- routes: int32 [4096, 4], P(('dp', 'expert')), may hold values from 0 to 7, as said below
- slots: int32 [4096, 4], P(('dp', 'expert')), may hold values from 0 to 127, as said below
- saved_hidden: bfloat16 [4, 8, 8, 128, 1440], P('dp', 'expert'), may hold values from -6 to 6
- left_wide: bfloat16 [8, 960, 960], P('expert', None, 'dp')
- left_narrow: bfloat16 [8, 480, 480], P('expert', None, 'dp')
- right_wide: bfloat16 [8, 960, 960], P('expert', None, 'dp')
- right_narrow: bfloat16 [8, 480, 480], P('expert', None, 'dp')
Outputs:
- precond_wide: float32 [8, 1440, 960], P('expert', None, 'dp')
- precond_narrow: float32 [8, 1440, 480], P('expert', None, 'dp')
The draws below stay inside these ranges and needn't reach their ends.
Inputs may be any that keep to these rules, and one draw needn't show every extreme that they name: Each row names 4 different experts. On each device the experts fall into groups of four and a token's routes name one whole group; no expert is named more than 128 times by the tokens of one device, and one expert is named exactly 128 times by the tokens of every device. slots[t, k] is the row of route k of token t in the buffer of 128 rows that its device fills for that expert; the routes of one device to one expert have different slots.
All inputs are finite; a program needn't handle non-finite values.
Results may differ from the reference program's by a relative error of at most 0.024.
Values may be sent and summed in bfloat16 or wider, within the bound.
No kernel may reach another device: no remote copies, remote signals or barrier semaphores. Data moves between devices by JAX's collectives and lax.ppermute only.
A program may use at most 64 MiB of HBM per device.

```python
import math
import jax
import jax.numpy as jnp
from jax import lax

TOK_DEV = 128
TOPK = 4
FFN = 1440
DMODEL = 1440
BLOCK = 960
REM_F = 480
REM_D = 480
EXPERTS = 8
SOURCES = 8
CAP = 128
TOKENS = 4096
N_DP = 4


def device_routes(device_key, hot_expert):
    key_order, key_place, key_turn, key_slots = jax.random.split(device_key, 4)
    groups = EXPERTS // 4
    virtual_order = jax.random.permutation(key_order, EXPERTS).astype(jnp.int32)
    hot_place = jnp.argmax(virtual_order == hot_expert)
    leading = virtual_order[0]
    virtual_order = virtual_order.at[hot_place].set(leading).at[0].set(hot_expert)
    full_class = min(CAP, TOK_DEV)
    remaining = TOK_DEV - full_class
    class_index = jnp.arange(groups, dtype=jnp.int32)
    others = remaining // (groups - 1) + (class_index - 1 < remaining % (groups - 1)).astype(jnp.int32)
    class_size = jnp.where(class_index == 0, full_class, others).astype(jnp.int32)
    class_end = jnp.cumsum(class_size)
    class_start = class_end - class_size
    placement = jax.random.permutation(key_place, TOK_DEV).astype(jnp.int32)
    token_class = jnp.sum((placement[:, None] >= class_end[None, :]).astype(jnp.int32), axis=1)
    class_rank = placement - class_start[token_class]
    rotation = jax.random.randint(key_turn, (TOK_DEV,), 0, 4)
    route_index = jnp.arange(4, dtype=jnp.int32)
    virtual = token_class[:, None] + groups * ((rotation[:, None] + route_index[None, :]) % 4)
    routes_here = virtual_order[virtual]

    def slot_order(slot_key):
        return jax.random.permutation(slot_key, CAP).astype(jnp.int32)
    slot_tables = jax.vmap(slot_order)(jax.random.split(key_slots, EXPERTS))
    slots_here = slot_tables[virtual, class_rank[:, None]]
    return (routes_here.astype(jnp.int32), slots_here.astype(jnp.int32))


def route_table(key):
    key_hot, key_device = jax.random.split(key)
    hot_expert = jax.random.randint(key_hot, (), 0, EXPERTS).astype(jnp.int32)
    device_keys = jax.random.split(key_device, TOKENS // TOK_DEV)
    routes_all, slots_all = jax.vmap(device_routes, in_axes=(0, None))(device_keys, hot_expert)
    return (routes_all.reshape(TOKENS, 4), slots_all.reshape(TOKENS, 4))


def symmetric_root(key, count, size, off_scale, diag_low):
    key_off, key_diag = jax.random.split(key)
    normals = jnp.clip(jax.random.normal(key_off, (count, size, size), jnp.float32), -4.0, 4.0)
    mirrored = (normals + jnp.swapaxes(normals, 1, 2)) * (off_scale / math.sqrt(2.0 * size))
    identity = jnp.eye(size, dtype=jnp.float32)
    diagonal = jax.random.uniform(key_diag, (count, size, 1), jnp.float32, diag_low, 2.0)
    return (mirrored * (1.0 - identity) + identity * diagonal).astype(jnp.bfloat16)


def draw_routes(key, part):
    table = route_table(key)
    return table[0]


def draw_slots(key, part):
    table = route_table(key)
    return table[1]


def draw_left_wide(key, part):
    key = jax.random.fold_in(key, 11)
    return symmetric_root(key, EXPERTS, BLOCK, 0.4, 1.0)


def draw_left_narrow(key, part):
    key = jax.random.fold_in(key, 12)
    return symmetric_root(key, EXPERTS, REM_F, 0.4, 1.0)


def draw_right_wide(key, part):
    key = jax.random.fold_in(key, 13)
    return symmetric_root(key, EXPERTS, BLOCK, 0.4, 1.0)


def draw_right_narrow(key, part):
    key = jax.random.fold_in(key, 14)
    return symmetric_root(key, EXPERTS, REM_D, 0.4, 1.0)


def levels(rng, dims, cuts, least, largest):
    def one(position, blocks):
        steps = jax.random.uniform(jax.random.fold_in(jax.random.fold_in(rng, 6), position), (blocks,), jnp.float32, least / len(cuts), largest / len(cuts))
        return jnp.repeat(jnp.exp(steps), dims[position] // blocks).reshape((-1,) + (1,) * (len(dims) - position - 1))

    factor_of = one(*cuts[0])
    for cut in cuts[1:]:
        factor_of = factor_of * one(*cut)
    return factor_of


def bell_draw(stream_key, dims, deviation, most, shards=(), kind=jnp.bfloat16):
    result = deviation * jax.random.normal(stream_key, dims, jnp.float32)
    if shards:
        result = result * levels(stream_key, dims, shards, -0.22, 0.18)
    return jnp.clip(result, -most, most).astype(kind)


def setup_inputs(seed: int = 0) -> dict:
    arg_keys = jax.random.split(jax.random.key(seed), 10)
    cotangent = bell_draw(arg_keys[0], (TOKENS, DMODEL), 0.01, 0.0625, ((0, 32),))
    gates = jnp.clip(0.049804688 + 0.54785156 * jax.random.uniform(arg_keys[1], (TOKENS, TOPK), jnp.float32) ** levels(arg_keys[1], (TOKENS, TOPK), ((0, 32),), -0.2, 0.2), 0.049804688, 0.59765625).astype(jnp.bfloat16)
    routes = draw_routes(jax.random.fold_in(arg_keys[9], 71), 0)
    slots = draw_slots(jax.random.fold_in(arg_keys[9], 71), 0)
    saved_hidden = bell_draw(arg_keys[4], (N_DP, EXPERTS, SOURCES, CAP, FFN), 1.0, 6.0, ((0, 4), (1, 8)))
    left_wide = draw_left_wide(jax.random.fold_in(arg_keys[9], 71), 0)
    left_narrow = draw_left_narrow(jax.random.fold_in(arg_keys[9], 71), 0)
    right_wide = draw_right_wide(jax.random.fold_in(arg_keys[9], 71), 0)
    right_narrow = draw_right_narrow(jax.random.fold_in(arg_keys[9], 71), 0)
    return dict(cotangent=cotangent, gates=gates, routes=routes, slots=slots, saved_hidden=saved_hidden, left_wide=left_wide, left_narrow=left_narrow, right_wide=right_wide, right_narrow=right_narrow)


def row_partial(cotangent_rows, gate_rows, route_rows, slot_rows, hidden_rows):
    scaled_rows = (gate_rows.astype(jnp.float32)[:, :, None] * cotangent_rows.astype(jnp.float32)[:, None, :]).astype(jnp.bfloat16)
    source_index = (jnp.arange(cotangent_rows.shape[0], dtype=jnp.int32) // TOK_DEV)[:, None]
    target = ((route_rows * SOURCES + source_index) * CAP + slot_rows).reshape(-1)
    buffer = jnp.zeros((EXPERTS * SOURCES * CAP, DMODEL), jnp.bfloat16).at[target].set(scaled_rows.reshape(-1, DMODEL))
    buffer = buffer.reshape(EXPERTS, SOURCES * CAP, DMODEL).astype(jnp.float32)
    hidden = hidden_rows.reshape(EXPERTS, SOURCES * CAP, FFN).astype(jnp.float32)
    partial_value = jnp.einsum("erh,erd->ehd", hidden, buffer)
    return partial_value.astype(jnp.bfloat16)


def reference(cotangent, gates, routes, slots, saved_hidden, left_wide, left_narrow, right_wide, right_narrow):
    row_tokens = TOK_DEV * SOURCES
    cotangent_rows = cotangent.reshape(N_DP, row_tokens, DMODEL)
    gate_rows = gates.reshape(N_DP, row_tokens, TOPK)
    route_rows = routes.reshape(N_DP, row_tokens, TOPK)
    slot_rows = slots.reshape(N_DP, row_tokens, TOPK)

    def accumulate(running, pieces):
        partial_value = lax.optimization_barrier(row_partial(*pieces))
        return running + partial_value.astype(jnp.float32), None

    gradient, _ = lax.scan(accumulate, jnp.zeros((EXPERTS, FFN, DMODEL), jnp.float32),
                           (cotangent_rows, gate_rows, route_rows, slot_rows, saved_hidden))
    gradient_bf = lax.optimization_barrier(gradient.astype(jnp.bfloat16)).astype(jnp.float32)
    precise = lax.Precision.HIGHEST
    right_product = jnp.concatenate([
        jnp.einsum("ehb,ebc->ehc", gradient_bf[:, :, :BLOCK], right_wide.astype(jnp.float32), precision=precise),
        jnp.einsum("ehb,ebc->ehc", gradient_bf[:, :, BLOCK:], right_narrow.astype(jnp.float32), precision=precise)], axis=2)
    right_bf = lax.optimization_barrier(right_product.astype(jnp.bfloat16)).astype(jnp.float32)
    stacked = jnp.concatenate([
        jnp.einsum("eab,ebd->ead", left_wide.astype(jnp.float32), right_bf[:, :BLOCK, :], precision=precise),
        jnp.einsum("eab,ebd->ead", left_narrow.astype(jnp.float32), right_bf[:, BLOCK:, :], precision=precise)], axis=1)
    return stacked[:, :, :BLOCK], stacked[:, :, BLOCK:]
```

```python
import functools

import jax
import jax.numpy as jnp
from jax import lax
from jax.experimental import pallas as pl
from jax.experimental.pallas import tpu as pltpu
from jax.sharding import PartitionSpec as P

BF16 = jnp.bfloat16
F32 = jnp.float32
LANES = 128
META_ROWS = 16
ROW_CHUNKS = 3
MIB = 1024 * 1024


def round_up(value, unit):
    return (value + unit - 1) // unit * unit


def params(mib):
    return pltpu.CompilerParams(vmem_limit_bytes=mib * MIB)


def cost():
    return pl.CostEstimate(flops=0, bytes_accessed=0, transcendentals=0)


class Order:
    def __init__(self, tick):
        self.tick = tick

    def gate(self, ready, values):
        self.tick, _, values = lax.optimization_barrier((self.tick, ready, values))
        return values


def dot_nn(left, right):
    return lax.dot_general(left, right, (((1,), (0,)), ((), ())), preferred_element_type=F32)


def dot_nt(left, right):
    return lax.dot_general(left, right, (((1,), (1,)), ((), ())), preferred_element_type=F32)


ANY = pl.BlockSpec(memory_space=pl.ANY)
VMEM = pl.BlockSpec(memory_space=pltpu.VMEM)


class Fold:
    def __init__(self, rows_w, rows_n, wide, narrow):
        self.rows_w, self.rows_n, self.wide, self.narrow = rows_w, rows_n, wide, narrow
        self.lanes = round_up(wide, LANES)
        self.step = round_up(narrow, LANES)
        self.ways = max(1, self.lanes // self.step)
        while rows_n % (self.ways * 16):
            self.ways -= 1
        self.part = rows_n // self.ways
        self.rows = rows_w + self.part
        self.shape = (self.rows, self.lanes)

    def write(self, ref, wide_value, narrow_value):
        ref[...] = jnp.zeros(self.shape, ref.dtype)
        ref[0 : self.rows_w, 0 : self.wide] = wide_value
        for way in range(self.ways):
            start = way * self.step
            ref[self.rows_w : self.rows, start : start + self.narrow] = narrow_value[
                way * self.part : (way + 1) * self.part
            ]

    def wide_of(self, value):
        return value[0 : self.rows_w, 0 : self.wide]

    def narrow_of(self, value):
        low = value[self.rows_w : self.rows]
        parts = [low[:, way * self.step : way * self.step + self.narrow] for way in range(self.ways)]
        return parts[0] if self.ways == 1 else jnp.concatenate(parts, axis=0)


def token_kernel(cot_ref, gate_ref, route_ref, slot_ref, tok_ref, gate, route, slot, meta, sem):
    width = cot_ref.shape[0]
    ways = gate_ref.shape[0]
    targets = (tok_ref.at[pl.ds(0, width)], gate, route, slot)
    copies = [
        pltpu.make_async_copy(source, target, sem.at[i])
        for i, (source, target) in enumerate(zip((cot_ref, gate_ref, route_ref, slot_ref), targets))
    ]
    for copy in copies:
        copy.start()
    for copy in copies[1:]:
        copy.wait()
    meta[...] = jnp.zeros(meta.shape, F32)
    meta[0:ways, :] = gate[...].astype(F32)
    meta[ways : 2 * ways, :] = route[...].astype(F32)
    meta[2 * ways : 3 * ways, :] = slot[...].astype(F32)
    tok_ref[width : width + META_ROWS, :] = meta[...].astype(BF16)
    copies[0].wait()


def pack_left_kernel(root, lw_ref, ln_ref, out_ref, wide, narrow, sem):
    copies = [
        pltpu.make_async_copy(lw_ref, wide, sem.at[0]),
        pltpu.make_async_copy(ln_ref, narrow, sem.at[1]),
    ]
    for copy in copies:
        copy.start()
    for copy in copies:
        copy.wait()
    root.write(out_ref, wide[...], narrow[...])


def partial_kernel(topk, width, low, high, hidden_ref, mine_ref, theirs_ref, out_ref, rows_ref):
    sources, _, capacity = hidden_ref.shape
    expert = lax.axis_index("expert")

    @pl.when(pl.program_id(0) == 0)
    def _():
        for offset in range(sources):
            token_ref = (mine_ref, theirs_ref)[offset % 2].at[offset // 2]
            source = jnp.bitwise_xor(expert, offset)
            meta = token_ref[width : width + META_ROWS, :].astype(F32)
            tokens = meta.shape[1]
            place = lax.broadcasted_iota(jnp.int32, (capacity, tokens), 0).astype(F32)
            here = expert.astype(F32)
            weights = jnp.zeros((capacity, tokens), F32)
            for k in range(topk):
                gate = meta[k : k + 1, :]
                route = meta[topk + k : topk + k + 1, :]
                slot = meta[2 * topk + k : 2 * topk + k + 1, :]
                wanted = jnp.where(route == here, slot, -1.0)
                weights = jnp.where(place == wanted, gate, weights)
            rows = pl.ds(pl.multiple_of(source * capacity, capacity), capacity)
            rows_ref[rows, :] = dot_nt(weights.astype(BF16), token_ref[low:high, :]).astype(BF16)

    if capacity % LANES == 0:
        hidden = jnp.concatenate([hidden_ref[s] for s in range(sources)], axis=1)
        out_ref[...] = dot_nn(hidden, rows_ref[...]).astype(BF16)
    else:
        total = dot_nn(hidden_ref[0], rows_ref[0:capacity, :])
        for s in range(1, sources):
            total += dot_nn(hidden_ref[s], rows_ref[s * capacity : (s + 1) * capacity, :])
        out_ref[...] = total.astype(BF16)


def sends(n, t, s):
    z = lax.axis_index("dp")
    up = z % 2 == s
    return jnp.where(up, (z <= t - 1) & (z < n - 1), z >= max(1, n - t))


def product_kernel(n, t, sets, partial_ref, *refs):
    count = len(refs) // 2
    rows = partial_ref.shape[0] // ROW_CHUNKS

    def product(root_ref, out_ref):
        for i in range(ROW_CHUNKS):
            part = slice(i * rows, (i + 1) * rows)
            out_ref[part, :] = dot_nn(partial_ref[part, :], root_ref[...]).astype(BF16)

    for i in range(count):
        make = functools.partial(product, refs[i], refs[count + i])
        if i < len(sets):
            pl.when(sends(n, t, sets[i]))(make)
        else:
            make()


def add_kernel(n, t, s, term_ref, got_ref, out_ref):
    @pl.when(sends(n, t, s))
    def _():
        out_ref[...] = (term_ref[...].astype(F32) + got_ref[...].astype(F32)).astype(BF16)


def left_kernel(root, n, own_ref, ends_ref, rest_ref, odd_ref, *refs):
    got = refs[: 2 * (n - 2)]
    wide_ref, narrow_ref, held, sem = refs[2 * (n - 2) :]
    z = lax.axis_index("dp")
    for here in range(n):
        even_ref = ends_ref if here in (1, n - 2) else rest_ref
        near = (even_ref, odd_ref) + got

        @pl.when(z == here)
        def _():
            copies = [pltpu.make_async_copy(own_ref, held.at[here], sem.at[here])]
            for q in range(n):
                if q != here:
                    s = here % 2 if q > here else 1 - here % 2
                    copies.append(
                        pltpu.make_async_copy(near[2 * (abs(q - here) - 1) + s], held.at[q], sem.at[q])
                    )
            for copy in copies:
                copy.start()
            for copy in copies:
                copy.wait()

    for q in range(n):
        piece = held[q]
        wide_ref[:, q * root.wide : (q + 1) * root.wide] = root.wide_of(piece)
        narrow_ref[:, q * root.narrow : (q + 1) * root.narrow] = root.narrow_of(piece)


def final_kernel(block, count, own_ref, *refs):
    wide_ref, narrow_ref, out_ref = refs[count:]
    rows = own_ref[...].astype(F32)
    for got_ref in refs[:count]:
        rows += got_ref[...].astype(F32)
    rows = rows.astype(BF16)
    out_ref[0:block, :] = dot_nn(wide_ref[...], rows[0:block])
    out_ref[block:, :] = dot_nn(narrow_ref[...], rows[block:])


def collect_kernel(count, *refs):
    sem = refs[-1]
    out_ref = refs[count]
    copies = [pltpu.make_async_copy(refs[i], out_ref.at[i], sem.at[i]) for i in range(count)]
    for copy in copies:
        copy.start()
    for copy in copies:
        copy.wait()


def body(
    cotangent, gates, routes, slots, saved_hidden, left_wide, left_narrow, right_wide, right_narrow
):
    tokens, width = cotangent.shape
    topk = gates.shape[1]
    n = lax.axis_size("dp")
    experts = lax.axis_size("expert")
    _, _, sources, capacity, ffn = saved_hidden.shape
    block, wide = right_wide.shape[1:]
    rest, narrow = right_narrow.shape[1:]
    root = Fold(block, rest, wide, narrow)

    def gather_pairs(k, s):
        up = [(i, i + 1) for i in range(s, n - 1, 2) if i >= k - 1]
        return up + [(i + 1, i) for i in range(s, n - 1, 2) if i <= n - 1 - k]

    def sum_pairs(t, s):
        up = [(i, i + 1) for i in range(s, n - 1, 2) if i <= t - 1]
        return up + [(i + 1, i) for i in range(s, n - 1, 2) if i + 1 >= n - t]

    def hop(k, pieces):
        return [
            lax.ppermute(pieces[1 - s], "dp", gather_pairs(k, s)) if gather_pairs(k, s) else pieces[1 - s]
            for s in (0, 1)
        ]

    tok = pl.pallas_call(
        token_kernel,
        in_specs=[ANY] * 4,
        out_specs=VMEM,
        out_shape=jax.ShapeDtypeStruct((width + META_ROWS, tokens), BF16),
        scratch_shapes=[
            pltpu.VMEM((topk, tokens), BF16),
            pltpu.VMEM((topk, tokens), jnp.int32),
            pltpu.VMEM((topk, tokens), jnp.int32),
            pltpu.VMEM((META_ROWS, tokens), F32),
            pltpu.SemaphoreType.DMA((4,)),
        ],
        compiler_params=params(56),
        cost_estimate=cost(),
        name="tokens",
    )(cotangent.T, gates.T, routes.T, slots.T)
    chips = experts // 2

    def collect(values):
        return pl.pallas_call(
            functools.partial(collect_kernel, chips),
            in_specs=[ANY] * chips,
            out_specs=ANY,
            out_shape=jax.ShapeDtypeStruct((chips,) + tok.shape, BF16),
            scratch_shapes=[pltpu.SemaphoreType.DMA((chips,))],
            compiler_params=params(16),
            cost_estimate=cost(),
            name="collect",
        )(*values)

    def pack_left(wide_piece, narrow_piece):
        return pl.pallas_call(
            functools.partial(pack_left_kernel, root),
            in_specs=[ANY] * 2,
            out_shape=jax.ShapeDtypeStruct(root.shape, BF16),
            scratch_shapes=[
                pltpu.VMEM((block, wide), BF16),
                pltpu.VMEM((rest, narrow), BF16),
                pltpu.SemaphoreType.DMA((2,)),
            ],
            compiler_params=params(16),
            cost_estimate=cost(),
            name="pack_left",
        )(wide_piece, narrow_piece)

    chunk_rows = ffn // ROW_CHUNKS
    hidden = jnp.swapaxes(saved_hidden[0, 0], 1, 2)

    def partial(low, high, mine, theirs):
        return pl.pallas_call(
            functools.partial(partial_kernel, topk, width, low, high),
            grid=(ROW_CHUNKS,),
            in_specs=[pl.BlockSpec((sources, chunk_rows, capacity), lambda i: (0, i, 0)), VMEM, VMEM],
            out_specs=pl.BlockSpec((chunk_rows, high - low), lambda i: (i, 0)),
            out_shape=jax.ShapeDtypeStruct((ffn, high - low), BF16),
            scratch_shapes=[pltpu.VMEM((sources * capacity, high - low), BF16)],
            compiler_params=params(24),
            cost_estimate=cost(),
            name="partial",
        )(hidden, mine, theirs)

    def product(value, t, got):
        sets = [s for s in (0, 1) if sum_pairs(t, s)]
        pieces = [got[n - t][s] for s in sets] + ([got[0][0]] if t == n - 1 else [])
        columns = pieces[0].shape[1]
        made = pl.pallas_call(
            functools.partial(product_kernel, n, t, sets),
            in_specs=[VMEM] * (1 + len(pieces)),
            out_specs=[VMEM] * len(pieces),
            out_shape=[jax.ShapeDtypeStruct((ffn, columns), BF16)] * len(pieces),
            compiler_params=params(16),
            cost_estimate=cost(),
            name="product",
        )(value, *pieces)
        return dict(zip(sets + [2], made))

    def add(t, s, term, got):
        return pl.pallas_call(
            functools.partial(add_kernel, n, t, s),
            in_specs=[VMEM] * 2,
            out_specs=VMEM,
            out_shape=jax.ShapeDtypeStruct(term.shape, BF16),
            compiler_params=params(16),
            cost_estimate=cost(),
            name="add",
        )(term, got)

    def send_sums(t, terms, last):
        sent = {}
        for s in (0, 1):
            if sum_pairs(t, s):
                term = terms[s]
                if 1 - s in last:
                    term = add(t, s, term, last[1 - s])
                sent[s] = lax.ppermute(term, "dp", sum_pairs(t, s))
        return sent

    order = Order(slots)
    mine = [tok] + [None] * (chips - 1)

    def exchange(value, steps):
        for m in steps:
            mine[m] = lax.ppermute(value, "expert", [(i, i ^ (2 * m)) for i in range(experts)])

    straight = [m for m in range(1, chips) if m & (m - 1) == 0]
    exchange(tok, straight)
    near = [[right_narrow[0]] * 2]
    for k in range(1, 3):
        near.append(hop(k, near[-1]))
    near[2], right_far, tok, left_wide, left_narrow = order.gate(
        [mine[m] for m in straight], (near[2], right_wide[0], tok, left_wide, left_narrow)
    )

    exchange(tok, [m for m in range(1, chips) if m not in straight])
    for k in range(3, n):
        near.append(hop(k, near[-1]))
    far = [[right_far] * 2]
    far.append(hop(1, far[0]))
    left = pack_left(left_wide[0], left_narrow[0])
    mine, near, far[1], left = order.gate((), (mine, near, far[1], left))

    mine = collect(mine)
    theirs = lax.ppermute(mine, "expert", [(i, i ^ 1) for i in range(experts)])
    far.append(hop(2, far[1]))
    ends = [pair for pair in gather_pairs(1, 0) if pair in ((0, 1), (n - 1, n - 2))]
    others = [pair for pair in gather_pairs(1, 0) if pair not in ends]
    left_ends = lax.ppermute(left, "dp", ends)
    part_near = partial(block, width, mine, theirs)
    terms_near = {1: product(part_near, 1, near)}
    far, left, left_ends, terms_near, part_near, mine, theirs = order.gate(
        (), (far, left, left_ends, terms_near, part_near, mine, theirs)
    )

    sent_near = send_sums(1, terms_near[1], {})
    for k in range(3, n):
        far.append(hop(k, far[-1]))
    left_odd = lax.ppermute(left, "dp", gather_pairs(1, 1))
    part_far = partial(0, block, mine, theirs)
    for t in range(2, n):
        terms_near[t] = product(part_near, t, near)
    terms_far = {1: product(part_far, 1, far)}
    far, part_far, terms_near, terms_far, sent_near, left, left_odd = order.gate(
        (), (far, part_far, terms_near, terms_far, sent_near, left, left_odd)
    )

    sent_far = send_sums(1, terms_far[1], {})
    sent_near = send_sums(2, terms_near[2], sent_near)
    left_rest = lax.ppermute(left, "dp", others) if others else left
    inner = {target for _, target in ends}
    z = lax.axis_index("dp")
    if all(pair[0] in inner for pair in gather_pairs(2, 1)):
        left_even = left_ends
    else:
        left_even = jnp.where((z == 1) | (z == n - 2), left_ends, left_rest)
    lefts = [[left, left], [left_even, left_odd]]
    lefts.append(hop(2, [left_even, lax.optimization_barrier((left_odd, left_rest))[0]]))
    for t in range(2, n):
        terms_far[t] = product(part_far, t, far)
    sent_far, sent_near, terms_far, left_rest, lefts[2] = order.gate(
        (), (sent_far, sent_near, terms_far, left_rest, lefts[2])
    )

    for t in range(2, n):
        sent_far = send_sums(t, terms_far[t], sent_far)
        if t + 1 < n:
            sent_near = send_sums(t + 1, terms_near[t + 1], sent_near)
            lefts.append(hop(t + 1, lefts[-1]))
            sent_far, sent_near, lefts[-1] = order.gate((), (sent_far, sent_near, lefts[-1]))

    left_inputs = [left, left_ends, left_rest, left_odd] + [value for pair in lefts[2:] for value in pair]
    left_w, left_n = pl.pallas_call(
        functools.partial(left_kernel, root, n),
        in_specs=[ANY] * len(left_inputs),
        out_shape=(
            jax.ShapeDtypeStruct((block, block), BF16),
            jax.ShapeDtypeStruct((rest, rest), BF16),
        ),
        scratch_shapes=[pltpu.VMEM((n,) + root.shape, BF16), pltpu.SemaphoreType.DMA((n,))],
        compiler_params=params(32),
        cost_estimate=cost(),
        name="left",
    )(*left_inputs)

    outs = []
    for terms, last in ((terms_near, sent_near), (terms_far, sent_far)):
        own = terms[n - 1][2]
        got = [last[s] for s in sorted(last)]
        outs.append(
            pl.pallas_call(
                functools.partial(final_kernel, block, len(got)),
                in_specs=[VMEM] * (3 + len(got)),
                out_specs=VMEM,
                out_shape=jax.ShapeDtypeStruct(own.shape, F32),
                compiler_params=params(32),
                cost_estimate=cost(),
                name="final",
            )(own, *got, left_w, left_n)[None]
        )
    return outs[1], outs[0]


def solution(mesh):
    return jax.shard_map(
        body,
        mesh=mesh,
        in_specs=(
            P(("dp", "expert"), None),
            P(("dp", "expert"), None),
            P(("dp", "expert"), None),
            P(("dp", "expert"), None),
            P("dp", "expert", None, None, None),
            P("expert", None, "dp"),
            P("expert", None, "dp"),
            P("expert", None, "dp"),
            P("expert", None, "dp"),
        ),
        out_specs=(P("expert", None, "dp"), P("expert", None, "dp")),
        check_vma=False,
    )
```

```python
import functools

import jax
import jax.numpy as jnp
from jax import lax
from jax.experimental import pallas as pl
from jax.experimental.pallas import tpu as pltpu
from jax.sharding import PartitionSpec as P

BF16 = jnp.bfloat16
F32 = jnp.float32
LANES = 128
META_ROWS = 16
ROW_CHUNKS = 3
MIB = 1024 * 1024


def round_up(value, unit):
    return (value + unit - 1) // unit * unit


def params(mib):
    return pltpu.CompilerParams(vmem_limit_bytes=mib * MIB)


def cost(micros=0):
    return pl.CostEstimate(flops=int(micros * 1.15e9), bytes_accessed=0, transcendentals=0)


class Order:
    def __init__(self, tick):
        self.tick = tick

    def gate(self, ready, values):
        self.tick, _, values = lax.optimization_barrier((self.tick, ready, values))
        return values


def dot_nn(left, right):
    return lax.dot_general(left, right, (((1,), (0,)), ((), ())), preferred_element_type=F32)


def dot_nt(left, right):
    return lax.dot_general(left, right, (((1,), (1,)), ((), ())), preferred_element_type=F32)


ANY = pl.BlockSpec(memory_space=pl.ANY)
VMEM = pl.BlockSpec(memory_space=pltpu.VMEM)


class Fold:
    def __init__(self, rows_w, rows_n, wide, narrow):
        self.rows_w, self.rows_n, self.wide, self.narrow = rows_w, rows_n, wide, narrow
        self.lanes = round_up(wide, LANES)
        self.step = round_up(narrow, LANES)
        self.ways = max(1, self.lanes // self.step)
        while rows_n % (self.ways * 16):
            self.ways -= 1
        self.part = rows_n // self.ways
        self.rows = rows_w + self.part
        self.shape = (self.rows, self.lanes)

    def write(self, ref, wide_value, narrow_value):
        ref[...] = jnp.zeros(self.shape, ref.dtype)
        ref[0 : self.rows_w, 0 : self.wide] = wide_value
        for way in range(self.ways):
            start = way * self.step
            ref[self.rows_w : self.rows, start : start + self.narrow] = narrow_value[
                way * self.part : (way + 1) * self.part
            ]

    def wide_of(self, value):
        return value[0 : self.rows_w, 0 : self.wide]

    def narrow_of(self, value):
        low = value[self.rows_w : self.rows]
        parts = [low[:, way * self.step : way * self.step + self.narrow] for way in range(self.ways)]
        return parts[0] if self.ways == 1 else jnp.concatenate(parts, axis=0)


def token_kernel(root, cot_ref, gate_ref, route_ref, slot_ref, rw_ref, rn_ref, tok_ref, right_ref,
                 gate, route, slot, wide, narrow, meta, sem):
    width = cot_ref.shape[0]
    ways = gate_ref.shape[0]
    sources = (rw_ref, rn_ref, gate_ref, route_ref, slot_ref, cot_ref)
    targets = (wide, narrow, gate, route, slot, tok_ref.at[pl.ds(0, width)])
    copies = [
        pltpu.make_async_copy(source, target, sem.at[i])
        for i, (source, target) in enumerate(zip(sources, targets))
    ]
    for copy in copies:
        copy.start()
    for copy in copies[:5]:
        copy.wait()
    root.write(right_ref, wide[...], narrow[...])
    meta[...] = jnp.zeros(meta.shape, F32)
    meta[0:ways, :] = gate[...].astype(F32)
    meta[ways : 2 * ways, :] = route[...].astype(F32)
    meta[2 * ways : 3 * ways, :] = slot[...].astype(F32)
    tok_ref[width : width + META_ROWS, :] = meta[...].astype(BF16)
    copies[5].wait()


def pack_left_kernel(root, lw_ref, ln_ref, out_ref, wide, narrow, sem):
    copies = [
        pltpu.make_async_copy(lw_ref, wide, sem.at[0]),
        pltpu.make_async_copy(ln_ref, narrow, sem.at[1]),
    ]
    for copy in copies:
        copy.start()
    for copy in copies:
        copy.wait()
    root.write(out_ref, wide[...], narrow[...])


def partial_kernel(topk, width, block, gap, first, later, hidden_ref, *refs):
    sources, _, capacity = hidden_ref.shape
    out_ref, rows_ref = refs[-2:]
    token_refs = {}
    for i, m in enumerate(first + later):
        token_refs[2 * m] = refs[i]
        if i < len(first):
            token_refs[2 * m + 1] = refs[len(first + later)].at[i]
        else:
            token_refs[2 * m + 1] = refs[len(first + later) + 1 + i - len(first)]
    expert = lax.axis_index("expert")
    parts = ((0, block, 0), (block, width, gap))

    @pl.when(pl.program_id(0) == 0)
    def _():
        for offset in range(sources):
            token_ref = token_refs[offset]
            source = jnp.bitwise_xor(expert, offset)
            meta = token_ref[width : width + META_ROWS, :].astype(F32)
            tokens = meta.shape[1]
            place = lax.broadcasted_iota(jnp.int32, (capacity, tokens), 0).astype(F32)
            here = expert.astype(F32)
            weights = jnp.zeros((capacity, tokens), F32)
            for k in range(topk):
                gate = meta[k : k + 1, :]
                route = meta[topk + k : topk + k + 1, :]
                slot = meta[2 * topk + k : 2 * topk + k + 1, :]
                wanted = jnp.where(route == here, slot, -1.0)
                weights = jnp.where(place == wanted, gate, weights)
            weights = weights.astype(BF16)
            rows = pl.ds(pl.multiple_of(source * capacity, capacity), capacity)
            for low, high, at in parts:
                value = dot_nt(weights, token_ref[low:high, :]).astype(BF16)
                rows_ref[rows, at : at + high - low] = value

    if capacity % LANES == 0:
        hidden = jnp.concatenate([hidden_ref[s] for s in range(sources)], axis=1)
    for low, high, at in parts:
        columns = slice(at, at + high - low)
        if capacity % LANES == 0:
            total = dot_nn(hidden, rows_ref[:, columns])
        else:
            total = dot_nn(hidden_ref[0], rows_ref[0:capacity, columns])
            for s in range(1, sources):
                total += dot_nn(hidden_ref[s], rows_ref[s * capacity : (s + 1) * capacity, columns])
        out_ref[:, columns] = total.astype(BF16)


class Chain:
    def __init__(self, n, half, order, low, fold):
        self.n, self.half, self.order, self.low, self.fold = n, half, order, low, fold
        self.steps = max(t for t in range(1, 2 * n) if self.pairs(t, 0) or self.pairs(t, 1))

    def distance(self, t, z, s):
        i = z if z % 2 == s else self.n - 1 - z
        if (z % 2 == s and z == self.n - 1) or (z % 2 != s and z == 0):
            return 0
        k = t - 1 - i
        if 0 <= k < len(self.order) and self.order[k] > i:
            return self.order[k] - i
        return 0

    def pairs(self, t, s):
        return [
            (z, z + 1 if z % 2 == s else z - 1) for z in range(self.n) if self.distance(t, z, s)
        ]

    def sets(self, t):
        return [s for s in (0, 1) if self.pairs(t, s)]

    def adds(self, t, s):
        targets = {target for _, target in self.pairs(t - 1, 1 - s)} if t > 1 else set()
        return any(z in targets for z, _ in self.pairs(t, s))

    def arrivals(self, z):
        found = []
        for t in range(1, self.steps + 1):
            for s in (0, 1):
                for sender, target in self.pairs(t, s):
                    if target == z and self.distance(t, sender, s) == 1:
                        found.append((t, s))
        return found


def product_kernel(chain, t, keys, root, block, gap, partial_ref, *refs):
    root_refs = dict(zip(keys, refs))
    out_refs, piece_ref = refs[len(keys) : -1], refs[-1]
    z = lax.axis_index("dp")
    fold = chain.fold

    def product(root_ref, out_ref):
        piece = root_ref[...]
        rows = slice(chain.low, chain.low + fold.rows_w)
        wide = dot_nn(partial_ref[rows, 0:block], root.wide_of(piece))
        narrow = dot_nn(partial_ref[rows, gap : gap + root.rows_n], root.narrow_of(piece))
        fold.write(out_ref, wide.astype(BF16), narrow.astype(BF16))

    def take(root_ref):
        piece_ref[...] = root_ref[...]

    if t == 0:
        product(root_refs[0, 0], out_refs[0])
        return
    for s, out_ref in zip(chain.sets(t), out_refs):
        by_far = {}
        for here in range(chain.n):
            far = chain.distance(t, here, s)
            if far:
                by_far[far] = by_far.get(far, False) | (z == here)
        if len(by_far) <= 2:
            for far, here in by_far.items():
                pl.when(here)(functools.partial(product, root_refs[far, s], out_ref))
        else:
            for far, here in by_far.items():
                pl.when(here)(functools.partial(take, root_refs[far, s]))
            here = functools.reduce(jnp.logical_or, by_far.values())
            pl.when(here)(functools.partial(product, piece_ref, out_ref))


def add_kernel(chain, t, s, term_ref, got_ref, out_ref):
    z = lax.axis_index("dp")
    sends = functools.reduce(jnp.logical_or, [z == here for here, _ in chain.pairs(t, s)])

    @pl.when(sends)
    def _():
        out_ref[...] = (term_ref[...].astype(F32) + got_ref[...].astype(F32)).astype(BF16)


def left_kernel(root, n, own_ref, ends_ref, rest_ref, odd_ref, *refs):
    got = refs[: 2 * (n - 2)]
    wide_ref, narrow_ref, held, sem = refs[2 * (n - 2) :]
    z = lax.axis_index("dp")
    for here in range(n):
        even_ref = ends_ref if here in (1, n - 2) else rest_ref
        near = (even_ref, odd_ref) + got

        @pl.when(z == here)
        def _():
            copies = [pltpu.make_async_copy(own_ref, held.at[here], sem.at[here])]
            for q in range(n):
                if q != here:
                    s = here % 2 if q > here else 1 - here % 2
                    copies.append(
                        pltpu.make_async_copy(near[2 * (abs(q - here) - 1) + s], held.at[q], sem.at[q])
                    )
            for copy in copies:
                copy.start()
            for copy in copies:
                copy.wait()

    for q in range(n):
        piece = held[q]
        wide_ref[:, q * root.wide : (q + 1) * root.wide] = root.wide_of(piece)
        narrow_ref[:, q * root.narrow : (q + 1) * root.narrow] = root.narrow_of(piece)


def add_arrivals(chains, got_refs, own_refs, out_refs, dtype):
    z = lax.axis_index("dp")
    for here in range(chains[0].n):

        @pl.when(z == here)
        def _():
            for chain, own_ref, out_ref in zip(chains, own_refs, out_refs):
                value = own_ref[...].astype(F32)
                for t, s in chain.arrivals(here):
                    if (chain.half, t, s) in got_refs:
                        value += got_refs[chain.half, t, s][...].astype(F32)
                out_ref[...] = value.astype(dtype)


def total_kernel(chains, keys, *refs):
    got_refs = dict(zip(keys, refs[len(chains) :]))
    add_arrivals(chains, got_refs, refs[: len(chains)], refs[len(chains) + len(keys) :], F32)


def final_kernel(chains, block, keys, *refs):
    got_refs = dict(zip(keys, refs[len(chains) :]))
    wide_ref, narrow_ref, out_w_ref, out_n_ref = refs[len(chains) + len(keys) :][:4]
    totals = refs[len(refs) - len(chains) :]
    add_arrivals(chains, got_refs, refs[: len(chains)], totals, BF16)
    wides = [chain.fold.wide_of(total[...]) for chain, total in zip(chains, totals)]
    narrows = [chain.fold.narrow_of(total[...]) for chain, total in zip(chains, totals)]
    for parts, out_ref in ((wides, out_w_ref), (narrows, out_n_ref)):
        rows = jnp.concatenate(parts, axis=0)
        out_ref[0:block, :] = dot_nn(wide_ref[...], rows[0:block])
        out_ref[block:, :] = dot_nn(narrow_ref[...], rows[block:])


def collect_kernel(count, *refs):
    sem = refs[-1]
    out_ref = refs[count]
    copies = [pltpu.make_async_copy(refs[i], out_ref.at[i], sem.at[i]) for i in range(count)]
    for copy in copies:
        copy.start()
    for copy in copies:
        copy.wait()


def body(
    cotangent, gates, routes, slots, saved_hidden, left_wide, left_narrow, right_wide, right_narrow
):
    tokens, width = cotangent.shape
    topk = gates.shape[1]
    n = lax.axis_size("dp")
    experts = lax.axis_size("expert")
    chips = experts // 2
    _, _, sources, capacity, ffn = saved_hidden.shape
    block, wide = right_wide.shape[1:]
    rest, narrow = right_narrow.shape[1:]
    gap = round_up(block, LANES)
    span = gap + round_up(rest, LANES)
    root = Fold(block, rest, wide, narrow)
    cut = ffn // 64 * 32
    folds = [Fold(rows, rows, wide, narrow) for rows in (cut, ffn - cut)]
    sooner = [n - 2, n - 1] if n > 2 else [1]
    chains = [
        Chain(n, 0, sooner + list(range(n - 3, 0, -1)), 0, folds[0]),
        Chain(n, 1, list(range(n - 1, 0, -1)), cut, folds[1]),
    ]

    def gather_pairs(k, s):
        up = [(i, i + 1) for i in range(s, n - 1, 2) if i >= k - 1]
        return up + [(i + 1, i) for i in range(s, n - 1, 2) if i <= n - 1 - k]

    def hop(k, pieces):
        return [
            lax.ppermute(pieces[1 - s], "dp", gather_pairs(k, s)) if gather_pairs(k, s) else pieces[1 - s]
            for s in (0, 1)
        ]

    tok, right = pl.pallas_call(
        functools.partial(token_kernel, root),
        in_specs=[ANY] * 6,
        out_specs=[VMEM] * 2,
        out_shape=[
            jax.ShapeDtypeStruct((width + META_ROWS, tokens), BF16),
            jax.ShapeDtypeStruct(root.shape, BF16),
        ],
        scratch_shapes=[
            pltpu.VMEM((topk, tokens), BF16),
            pltpu.VMEM((topk, tokens), jnp.int32),
            pltpu.VMEM((topk, tokens), jnp.int32),
            pltpu.VMEM((block, wide), BF16),
            pltpu.VMEM((rest, narrow), BF16),
            pltpu.VMEM((META_ROWS, tokens), F32),
            pltpu.SemaphoreType.DMA((6,)),
        ],
        compiler_params=params(56),
        cost_estimate=cost(),
        name="tokens",
    )(cotangent.T, gates.T, routes.T, slots.T, right_wide[0], right_narrow[0])

    def collect(values):
        count = len(values)
        return pl.pallas_call(
            functools.partial(collect_kernel, count),
            in_specs=[ANY] * count,
            out_specs=ANY,
            out_shape=jax.ShapeDtypeStruct((count,) + tok.shape, BF16),
            scratch_shapes=[pltpu.SemaphoreType.DMA((count,))],
            compiler_params=params(16),
            cost_estimate=cost(),
            name="collect",
        )(*values)

    def pack_left(wide_piece, narrow_piece):
        return pl.pallas_call(
            functools.partial(pack_left_kernel, root),
            in_specs=[ANY] * 2,
            out_shape=jax.ShapeDtypeStruct(root.shape, BF16),
            scratch_shapes=[
                pltpu.VMEM((block, wide), BF16),
                pltpu.VMEM((rest, narrow), BF16),
                pltpu.SemaphoreType.DMA((2,)),
            ],
            compiler_params=params(16),
            cost_estimate=cost(),
            name="pack_left",
        )(wide_piece, narrow_piece)

    chunk_rows = ffn // ROW_CHUNKS
    hidden = jnp.swapaxes(saved_hidden[0, 0], 1, 2)

    def partial(first, later, mine, theirs_first, theirs_later):
        return pl.pallas_call(
            functools.partial(partial_kernel, topk, width, block, gap, first, later),
            grid=(ROW_CHUNKS,),
            in_specs=[pl.BlockSpec((sources, chunk_rows, capacity), lambda i: (0, i, 0))]
            + [VMEM] * (1 + len(mine) + len(later)),
            out_specs=pl.BlockSpec((chunk_rows, span), lambda i: (i, 0)),
            out_shape=jax.ShapeDtypeStruct((ffn, span), BF16),
            scratch_shapes=[pltpu.VMEM((sources * capacity, span), BF16)],
            compiler_params=params(32),
            cost_estimate=cost(),
            name="partial",
        )(hidden, *mine, theirs_first, *theirs_later)

    def product(chain, t, value, got):
        keys = [(0, 0)]
        if t:
            keys = sorted({(chain.distance(t, z, s), s) for z in range(n) for s in (0, 1)})
            keys = [key for key in keys if key[0]]
        sets = chain.sets(t) if t else [0]
        made = pl.pallas_call(
            functools.partial(product_kernel, chain, t, keys, root, block, gap),
            in_specs=[VMEM] * (1 + len(keys)),
            out_specs=[VMEM] * len(sets),
            out_shape=[jax.ShapeDtypeStruct(chain.fold.shape, BF16)] * len(sets),
            scratch_shapes=[pltpu.VMEM(root.shape, BF16)],
            compiler_params=params(16),
            cost_estimate=cost(),
            name="product",
        )(value, *[got[far][s] for far, s in keys])
        return dict(zip(sets, made))

    def add(chain, t, s, term, got):
        return pl.pallas_call(
            functools.partial(add_kernel, chain, t, s),
            in_specs=[VMEM] * 2,
            out_specs=VMEM,
            out_shape=jax.ShapeDtypeStruct(term.shape, BF16),
            compiler_params=params(16),
            cost_estimate=cost(),
            name="add",
        )(term, got)

    order = Order(slots)
    straight = [m for m in range(1, chips) if m & (m - 1) == 0]
    mine = {0: tok}
    for m in straight:
        mine[m] = lax.ppermute(tok, "expert", [(i, i ^ (2 * m)) for i in range(experts)])
    got = [[right, right]]
    got.append(hop(1, got[0]))
    left = pack_left(left_wide[0], left_narrow[0])
    mine, got, left = order.gate((), (mine, got, left))

    first = [0] + straight
    later = [m for m in range(1, chips) if m not in straight]
    for m in later:
        mine[m] = lax.ppermute(mine[0], "expert", [(i, i ^ (2 * m)) for i in range(experts)])
    for k in range(2, n - 1):
        got.append(hop(k, got[-1]))

    def sibling(piece):
        return lax.ppermute(piece, "expert", [(i, i ^ 1) for i in range(experts)])

    theirs_first = sibling(collect([mine[m] for m in first]))
    ends = [pair for pair in gather_pairs(1, 0) if pair in ((0, 1), (n - 1, n - 2))]
    others = [pair for pair in gather_pairs(1, 0) if pair not in ends]
    left_ends = lax.ppermute(left, "dp", ends)
    theirs_later = [sibling(mine[m]) for m in later]
    value = partial(first, later, [mine[m] for m in first + later], theirs_first, theirs_later)
    got, left, left_ends, value = order.gate((), (got, left, left_ends, value))

    one, two = chains
    sent, terms = {}, {}

    def hop_one(pairs, piece):
        return lax.ppermute(piece, "dp", pairs) if pairs else piece

    def make(chain, t):
        terms[chain.half, t] = product(chain, t, value, got)

    def wait(keys, more=(), values=()):
        ready, _, values = order.gate((), ([sent[key] for key in keys], more, values))
        sent.update(zip(keys, ready))
        return values

    def go(chain, t, s):
        term = terms[chain.half, t][s]
        if chain.adds(t, s):
            term = add(chain, t, s, term, sent[chain.half, t - 1, 1 - s])
        sent[chain.half, t, s] = lax.ppermute(term, "dp", chain.pairs(t, s))

    make(one, 1)
    for s in one.sets(1):
        go(one, 1, s)
    for k in range(max(2, n - 1), n):
        got.append(hop(k, got[-1]))
    left_odd = hop_one(gather_pairs(1, 1), left)
    left_rest = hop_one(others, left)
    inner = {target for _, target in ends}
    if all(pair[0] in inner for pair in gather_pairs(2, 1)):
        left_even = left_ends
    else:
        z = lax.axis_index("dp")
        left_even = jnp.where((z == 1) | (z == n - 2), left_ends, left_rest)
    second = [None, hop_one(gather_pairs(2, 1), left_even)]
    own = [product(chain, 0, value, got)[0] for chain in chains]

    got, value, left_odd = wait([(0, 1, s) for s in one.sets(1)], (), (got, value, left_odd))
    make(two, 1)
    make(one, 2)
    for s in two.sets(1):
        go(two, 1, s)
    if n == 4:
        go(one, 2, 1)
        second[0] = hop_one(gather_pairs(2, 0), left_odd)
        left_rest, second[1], terms[0, 2] = wait([], (), (left_rest, second[1], terms[0, 2]))
        go(one, 2, 0)
        third = hop_one(gather_pairs(3, 0), second[1])
        make(two, 2)
        second[0], terms[1, 2] = wait([(1, 1, 0)], (), (second[0], terms[1, 2]))
        go(two, 2, 1)
        go(two, 2, 0)
        make(one, 3)
        terms[0, 3] = wait([(0, 2, 0), (0, 2, 1)], (), terms[0, 3])
        go(one, 3, 1)
        go(one, 3, 0)
        make(two, 3)
        third, terms[1, 3] = wait([(1, 2, 1)], (), (third, terms[1, 3]))
        go(two, 3, 0)
        make(one, 4)
        terms[0, 4], terms[1, 3] = wait([(0, 3, 1), (1, 2, 0)], (), (terms[0, 4], terms[1, 3]))
        go(one, 4, 0)
        go(two, 3, 1)
        lefts = [[left, left], [left_even, left_odd], second, [third, third]]
    else:
        for s in one.sets(2):
            go(one, 2, s)
        second[0] = hop_one(gather_pairs(2, 0), left_odd)
        lefts = [[left, left], [left_even, left_odd], second]
        for t in range(2, max(chain.steps for chain in chains) + 1):
            for chain in chains:
                if t <= chain.steps and (chain.half, t) != (0, 2):
                    make(chain, t)
                    before = [(chain.half, t - 1, s) for s in chain.sets(t - 1)]
                    terms[chain.half, t] = wait(before, (), terms[chain.half, t])
                    for s in chain.sets(t):
                        go(chain, t, s)
            if 2 < t < n:
                lefts.append(hop(t, wait([], (), lefts[-1])))

    left_inputs = [left, left_ends, left_rest, left_odd] + [item for pair in lefts[2:] for item in pair]
    left_w, left_n = pl.pallas_call(
        functools.partial(left_kernel, root, n),
        in_specs=[ANY] * len(left_inputs),
        out_shape=(
            jax.ShapeDtypeStruct((block, block), BF16),
            jax.ShapeDtypeStruct((rest, rest), BF16),
        ),
        scratch_shapes=[pltpu.VMEM((n,) + root.shape, BF16), pltpu.SemaphoreType.DMA((n,))],
        compiler_params=params(32),
        cost_estimate=cost(),
        name="left",
    )(*left_inputs)

    keys = sorted({(chain.half, t, s) for chain in chains for here in range(n) for t, s in chain.arrivals(here)})
    last = [(0, one.steps, s) for s in one.sets(one.steps)] + [(1, two.steps, 1)]
    early = [key for key in keys if key not in last]
    last = [key for key in keys if key in last]
    own = wait(early, (left_w, left_n), own)
    totals = pl.pallas_call(
        functools.partial(total_kernel, chains, early),
        in_specs=[VMEM] * (len(chains) + len(early)),
        out_specs=[VMEM] * len(chains),
        out_shape=[jax.ShapeDtypeStruct(chain.fold.shape, F32) for chain in chains],
        compiler_params=params(32),
        cost_estimate=cost(3),
        name="total",
    )(*own, *[sent[key] for key in early])
    out_w, out_n = pl.pallas_call(
        functools.partial(final_kernel, chains, block, last),
        in_specs=[VMEM] * (len(chains) + len(last) + 2),
        out_specs=[VMEM] * 2,
        out_shape=[jax.ShapeDtypeStruct((ffn, wide), F32), jax.ShapeDtypeStruct((ffn, narrow), F32)],
        scratch_shapes=[pltpu.VMEM(chain.fold.shape, BF16) for chain in chains],
        compiler_params=params(32),
        cost_estimate=cost(),
        name="final",
    )(*totals, *[sent[key] for key in last], left_w, left_n)
    return out_w[None], out_n[None]


def solution(mesh):
    return jax.shard_map(
        body,
        mesh=mesh,
        in_specs=(
            P(("dp", "expert"), None),
            P(("dp", "expert"), None),
            P(("dp", "expert"), None),
            P(("dp", "expert"), None),
            P("dp", "expert", None, None, None),
            P("expert", None, "dp"),
            P("expert", None, "dp"),
            P("expert", None, "dp"),
            P("expert", None, "dp"),
        ),
        out_specs=(P("expert", None, "dp"), P("expert", None, "dp")),
        check_vma=False,
    )
```

```python
import functools

import jax
import jax.numpy as jnp
from jax import lax
from jax.experimental import pallas as pl
from jax.experimental.pallas import tpu as pltpu
from jax.sharding import PartitionSpec as P

BF16 = jnp.bfloat16
F32 = jnp.float32
LANES = 128
META_ROWS = 16
ROW_CHUNKS = 3
MIB = 1024 * 1024


def round_up(value, unit):
    return (value + unit - 1) // unit * unit


def params(mib):
    return pltpu.CompilerParams(vmem_limit_bytes=mib * MIB)


def cost(micros=0):
    return pl.CostEstimate(flops=int(micros * 1.15e9), bytes_accessed=0, transcendentals=0)


class Order:
    def __init__(self, tick):
        self.tick = tick

    def gate(self, ready, values):
        self.tick, _, values = lax.optimization_barrier((self.tick, ready, values))
        return values


def dot_nn(left, right):
    return lax.dot_general(left, right, (((1,), (0,)), ((), ())), preferred_element_type=F32)


def dot_nt(left, right):
    return lax.dot_general(left, right, (((1,), (1,)), ((), ())), preferred_element_type=F32)


ANY = pl.BlockSpec(memory_space=pl.ANY)
VMEM = pl.BlockSpec(memory_space=pltpu.VMEM)


class Fold:
    def __init__(self, rows_w, rows_n, wide, narrow):
        self.rows_w, self.rows_n, self.wide, self.narrow = rows_w, rows_n, wide, narrow
        self.lanes = round_up(wide, LANES)
        self.step = round_up(narrow, LANES)
        self.ways = max(1, self.lanes // self.step)
        while rows_n % (self.ways * 16):
            self.ways -= 1
        self.part = rows_n // self.ways
        self.rows = rows_w + self.part
        self.shape = (self.rows, self.lanes)

    def write(self, ref, wide_value, narrow_value):
        ref[...] = jnp.zeros(self.shape, ref.dtype)
        ref[0 : self.rows_w, 0 : self.wide] = wide_value
        for way in range(self.ways):
            start = way * self.step
            ref[self.rows_w : self.rows, start : start + self.narrow] = narrow_value[
                way * self.part : (way + 1) * self.part
            ]

    def wide_of(self, value):
        return value[0 : self.rows_w, 0 : self.wide]

    def narrow_of(self, value):
        low = value[self.rows_w : self.rows]
        parts = [low[:, way * self.step : way * self.step + self.narrow] for way in range(self.ways)]
        return parts[0] if self.ways == 1 else jnp.concatenate(parts, axis=0)


def token_kernel(root, cot_ref, gate_ref, route_ref, slot_ref, rw_ref, rn_ref, tok_ref, right_ref,
                 gate, route, slot, wide, narrow, meta, sem):
    width = cot_ref.shape[0]
    ways = gate_ref.shape[0]
    sources = (rw_ref, rn_ref, gate_ref, route_ref, slot_ref, cot_ref)
    targets = (wide, narrow, gate, route, slot, tok_ref.at[pl.ds(0, width)])
    copies = [
        pltpu.make_async_copy(source, target, sem.at[i])
        for i, (source, target) in enumerate(zip(sources, targets))
    ]
    for copy in copies:
        copy.start()
    for copy in copies[:5]:
        copy.wait()
    root.write(right_ref, wide[...], narrow[...])
    meta[...] = jnp.zeros(meta.shape, F32)
    meta[0:ways, :] = gate[...].astype(F32)
    meta[ways : 2 * ways, :] = route[...].astype(F32)
    meta[2 * ways : 3 * ways, :] = slot[...].astype(F32)
    tok_ref[width : width + META_ROWS, :] = meta[...].astype(BF16)
    copies[5].wait()


def pack_left_kernel(root, lw_ref, ln_ref, out_ref, wide, narrow, sem):
    copies = [
        pltpu.make_async_copy(lw_ref, wide, sem.at[0]),
        pltpu.make_async_copy(ln_ref, narrow, sem.at[1]),
    ]
    for copy in copies:
        copy.start()
    for copy in copies:
        copy.wait()
    root.write(out_ref, wide[...], narrow[...])


def partial_kernel(topk, width, block, gap, first, later, hidden_ref, *refs):
    sources, _, capacity = hidden_ref.shape
    out_ref, rows_ref = refs[-2:]
    token_refs = {}
    for i, m in enumerate(first + later):
        token_refs[2 * m] = refs[i]
        if i < len(first):
            token_refs[2 * m + 1] = refs[len(first + later)].at[i]
        else:
            token_refs[2 * m + 1] = refs[len(first + later) + 1 + i - len(first)]
    expert = lax.axis_index("expert")
    parts = ((0, block, 0), (block, width, gap))

    @pl.when(pl.program_id(0) == 0)
    def _():
        for offset in range(sources):
            token_ref = token_refs[offset]
            source = jnp.bitwise_xor(expert, offset)
            meta = token_ref[width : width + META_ROWS, :].astype(F32)
            tokens = meta.shape[1]
            place = lax.broadcasted_iota(jnp.int32, (capacity, tokens), 0).astype(F32)
            here = expert.astype(F32)
            weights = jnp.zeros((capacity, tokens), F32)
            for k in range(topk):
                gate = meta[k : k + 1, :]
                route = meta[topk + k : topk + k + 1, :]
                slot = meta[2 * topk + k : 2 * topk + k + 1, :]
                wanted = jnp.where(route == here, slot, -1.0)
                weights = jnp.where(place == wanted, gate, weights)
            weights = weights.astype(BF16)
            rows = pl.ds(pl.multiple_of(source * capacity, capacity), capacity)
            for low, high, at in parts:
                value = dot_nt(weights, token_ref[low:high, :]).astype(BF16)
                rows_ref[rows, at : at + high - low] = value

    if capacity % LANES == 0:
        hidden = jnp.concatenate([hidden_ref[s] for s in range(sources)], axis=1)
    for low, high, at in parts:
        columns = slice(at, at + high - low)
        if capacity % LANES == 0:
            total = dot_nn(hidden, rows_ref[:, columns])
        else:
            total = dot_nn(hidden_ref[0], rows_ref[0:capacity, columns])
            for s in range(1, sources):
                total += dot_nn(hidden_ref[s], rows_ref[s * capacity : (s + 1) * capacity, columns])
        out_ref[:, columns] = total.astype(BF16)


class Chain:
    def __init__(self, n, half, order, low, fold):
        self.n, self.half, self.order, self.low, self.fold = n, half, order, low, fold
        self.steps = max(t for t in range(1, 2 * n) if self.pairs(t, 0) or self.pairs(t, 1))

    def distance(self, t, z, s):
        i = z if z % 2 == s else self.n - 1 - z
        if (z % 2 == s and z == self.n - 1) or (z % 2 != s and z == 0):
            return 0
        k = t - 1 - i
        if 0 <= k < len(self.order) and self.order[k] > i:
            return self.order[k] - i
        return 0

    def pairs(self, t, s):
        return [
            (z, z + 1 if z % 2 == s else z - 1) for z in range(self.n) if self.distance(t, z, s)
        ]

    def sets(self, t):
        return [s for s in (0, 1) if self.pairs(t, s)]

    def adds(self, t, s):
        targets = {target for _, target in self.pairs(t - 1, 1 - s)} if t > 1 else set()
        return any(z in targets for z, _ in self.pairs(t, s))

    def arrivals(self, z):
        found = []
        for t in range(1, self.steps + 1):
            for s in (0, 1):
                for sender, target in self.pairs(t, s):
                    if target == z and self.distance(t, sender, s) == 1:
                        found.append((t, s))
        return found


def product_kernel(chain, t, keys, root, block, gap, partial_ref, *refs):
    root_refs = dict(zip(keys, refs))
    out_refs, piece_ref = refs[len(keys) : -1], refs[-1]
    z = lax.axis_index("dp")
    fold = chain.fold

    def product(root_ref, out_ref):
        piece = root_ref[...]
        rows = slice(chain.low, chain.low + fold.rows_w)
        wide = dot_nn(partial_ref[rows, 0:block], root.wide_of(piece))
        narrow = dot_nn(partial_ref[rows, gap : gap + root.rows_n], root.narrow_of(piece))
        fold.write(out_ref, wide.astype(BF16), narrow.astype(BF16))

    def take(root_ref):
        piece_ref[...] = root_ref[...]

    if t == 0:
        product(root_refs[0, 0], out_refs[0])
        return
    for s, out_ref in zip(chain.sets(t), out_refs):
        by_far = {}
        for here in range(chain.n):
            far = chain.distance(t, here, s)
            if far:
                by_far[far] = by_far.get(far, False) | (z == here)
        if len(by_far) <= 2:
            for far, here in by_far.items():
                pl.when(here)(functools.partial(product, root_refs[far, s], out_ref))
        else:
            for far, here in by_far.items():
                pl.when(here)(functools.partial(take, root_refs[far, s]))
            here = functools.reduce(jnp.logical_or, by_far.values())
            pl.when(here)(functools.partial(product, piece_ref, out_ref))


def add_kernel(chain, t, s, term_ref, got_ref, out_ref):
    z = lax.axis_index("dp")
    sends = functools.reduce(jnp.logical_or, [z == here for here, _ in chain.pairs(t, s)])

    @pl.when(sends)
    def _():
        out_ref[...] = (term_ref[...].astype(F32) + got_ref[...].astype(F32)).astype(BF16)


def left_kernel(root, n, own_ref, ends_ref, rest_ref, odd_ref, *refs):
    got = refs[: 2 * (n - 2)]
    wide_ref, narrow_ref, held, sem = refs[2 * (n - 2) :]
    z = lax.axis_index("dp")
    for here in range(n):
        even_ref = ends_ref if here in (1, n - 2) else rest_ref
        near = (even_ref, odd_ref) + got

        @pl.when(z == here)
        def _():
            copies = [pltpu.make_async_copy(own_ref, held.at[here], sem.at[here])]
            for q in range(n):
                if q != here:
                    s = here % 2 if q > here else 1 - here % 2
                    copies.append(
                        pltpu.make_async_copy(near[2 * (abs(q - here) - 1) + s], held.at[q], sem.at[q])
                    )
            for copy in copies:
                copy.start()
            for copy in copies:
                copy.wait()

    for q in range(n):
        piece = held[q]
        wide_ref[:, q * root.wide : (q + 1) * root.wide] = root.wide_of(piece)
        narrow_ref[:, q * root.narrow : (q + 1) * root.narrow] = root.narrow_of(piece)


def add_arrivals(chains, got_refs, own_refs, out_refs, dtype):
    z = lax.axis_index("dp")
    for here in range(chains[0].n):

        @pl.when(z == here)
        def _():
            for chain, own_ref, out_ref in zip(chains, own_refs, out_refs):
                value = own_ref[...].astype(F32)
                for t, s in chain.arrivals(here):
                    if (chain.half, t, s) in got_refs:
                        value += got_refs[chain.half, t, s][...].astype(F32)
                out_ref[...] = value.astype(dtype)


def total_kernel(chains, keys, *refs):
    got_refs = dict(zip(keys, refs[len(chains) :]))
    add_arrivals(chains, got_refs, refs[: len(chains)], refs[len(chains) + len(keys) :], F32)


def final_kernel(chains, block, keys, *refs):
    got_refs = dict(zip(keys, refs[len(chains) :]))
    wide_ref, narrow_ref, out_w_ref, out_n_ref = refs[len(chains) + len(keys) :][:4]
    totals = refs[len(refs) - len(chains) :]
    add_arrivals(chains, got_refs, refs[: len(chains)], totals, BF16)
    wides = [chain.fold.wide_of(total[...]) for chain, total in zip(chains, totals)]
    narrows = [chain.fold.narrow_of(total[...]) for chain, total in zip(chains, totals)]
    for parts, out_ref in ((wides, out_w_ref), (narrows, out_n_ref)):
        rows = jnp.concatenate(parts, axis=0)
        out_ref[0:block, :] = dot_nn(wide_ref[...], rows[0:block])
        out_ref[block:, :] = dot_nn(narrow_ref[...], rows[block:])


def collect_kernel(count, *refs):
    sem = refs[-1]
    out_ref = refs[count]
    copies = [pltpu.make_async_copy(refs[i], out_ref.at[i], sem.at[i]) for i in range(count)]
    for copy in copies:
        copy.start()
    for copy in copies:
        copy.wait()


def body(
    cotangent, gates, routes, slots, saved_hidden, left_wide, left_narrow, right_wide, right_narrow
):
    tokens, width = cotangent.shape
    topk = gates.shape[1]
    n = lax.axis_size("dp")
    experts = lax.axis_size("expert")
    chips = experts // 2
    _, _, sources, capacity, ffn = saved_hidden.shape
    block, wide = right_wide.shape[1:]
    rest, narrow = right_narrow.shape[1:]
    gap = round_up(block, LANES)
    span = gap + round_up(rest, LANES)
    root = Fold(block, rest, wide, narrow)
    cut = ffn - ffn // 64 * 32
    folds = [Fold(rows, rows, wide, narrow) for rows in (cut, ffn - cut)]
    sooner = [n - 2, n - 1] if n > 2 else [1]
    sooner += list(range(n - 3, 0, -1))
    chains = [Chain(n, 0, sooner, 0, folds[0]), Chain(n, 1, sooner, cut, folds[1])]

    def gather_pairs(k, s):
        up = [(i, i + 1) for i in range(s, n - 1, 2) if i >= k - 1]
        return up + [(i + 1, i) for i in range(s, n - 1, 2) if i <= n - 1 - k]

    def hop(k, pieces):
        return [
            lax.ppermute(pieces[1 - s], "dp", gather_pairs(k, s)) if gather_pairs(k, s) else pieces[1 - s]
            for s in (0, 1)
        ]

    tok, right = pl.pallas_call(
        functools.partial(token_kernel, root),
        in_specs=[ANY] * 6,
        out_specs=[VMEM] * 2,
        out_shape=[
            jax.ShapeDtypeStruct((width + META_ROWS, tokens), BF16),
            jax.ShapeDtypeStruct(root.shape, BF16),
        ],
        scratch_shapes=[
            pltpu.VMEM((topk, tokens), BF16),
            pltpu.VMEM((topk, tokens), jnp.int32),
            pltpu.VMEM((topk, tokens), jnp.int32),
            pltpu.VMEM((block, wide), BF16),
            pltpu.VMEM((rest, narrow), BF16),
            pltpu.VMEM((META_ROWS, tokens), F32),
            pltpu.SemaphoreType.DMA((6,)),
        ],
        compiler_params=params(56),
        cost_estimate=cost(),
        name="tokens",
    )(cotangent.T, gates.T, routes.T, slots.T, right_wide[0], right_narrow[0])

    def collect(values):
        count = len(values)
        return pl.pallas_call(
            functools.partial(collect_kernel, count),
            in_specs=[ANY] * count,
            out_specs=ANY,
            out_shape=jax.ShapeDtypeStruct((count,) + tok.shape, BF16),
            scratch_shapes=[pltpu.SemaphoreType.DMA((count,))],
            compiler_params=params(16),
            cost_estimate=cost(),
            name="collect",
        )(*values)

    def pack_left(wide_piece, narrow_piece):
        return pl.pallas_call(
            functools.partial(pack_left_kernel, root),
            in_specs=[ANY] * 2,
            out_shape=jax.ShapeDtypeStruct(root.shape, BF16),
            scratch_shapes=[
                pltpu.VMEM((block, wide), BF16),
                pltpu.VMEM((rest, narrow), BF16),
                pltpu.SemaphoreType.DMA((2,)),
            ],
            compiler_params=params(16),
            cost_estimate=cost(),
            name="pack_left",
        )(wide_piece, narrow_piece)

    chunk_rows = ffn // ROW_CHUNKS
    hidden = jnp.swapaxes(saved_hidden[0, 0], 1, 2)

    def partial(first, later, mine, theirs_first, theirs_later):
        return pl.pallas_call(
            functools.partial(partial_kernel, topk, width, block, gap, first, later),
            grid=(ROW_CHUNKS,),
            in_specs=[pl.BlockSpec((sources, chunk_rows, capacity), lambda i: (0, i, 0))]
            + [VMEM] * (1 + len(mine) + len(later)),
            out_specs=pl.BlockSpec((chunk_rows, span), lambda i: (i, 0)),
            out_shape=jax.ShapeDtypeStruct((ffn, span), BF16),
            scratch_shapes=[pltpu.VMEM((sources * capacity, span), BF16)],
            compiler_params=params(32),
            cost_estimate=cost(),
            name="partial",
        )(hidden, *mine, theirs_first, *theirs_later)

    def product(chain, t, value, got):
        keys = [(0, 0)]
        if t:
            keys = sorted({(chain.distance(t, z, s), s) for z in range(n) for s in (0, 1)})
            keys = [key for key in keys if key[0]]
        sets = chain.sets(t) if t else [0]
        made = pl.pallas_call(
            functools.partial(product_kernel, chain, t, keys, root, block, gap),
            in_specs=[VMEM] * (1 + len(keys)),
            out_specs=[VMEM] * len(sets),
            out_shape=[jax.ShapeDtypeStruct(chain.fold.shape, BF16)] * len(sets),
            scratch_shapes=[pltpu.VMEM(root.shape, BF16)],
            compiler_params=params(16),
            cost_estimate=cost(),
            name="product",
        )(value, *[got[far][s] for far, s in keys])
        return dict(zip(sets, made))

    def add(chain, t, s, term, got):
        return pl.pallas_call(
            functools.partial(add_kernel, chain, t, s),
            in_specs=[VMEM] * 2,
            out_specs=VMEM,
            out_shape=jax.ShapeDtypeStruct(term.shape, BF16),
            compiler_params=params(16),
            cost_estimate=cost(),
            name="add",
        )(term, got)

    order = Order(slots)
    straight = [m for m in range(1, chips) if m & (m - 1) == 0]
    mine = {0: tok}
    for m in straight:
        mine[m] = lax.ppermute(tok, "expert", [(i, i ^ (2 * m)) for i in range(experts)])
    got = [[right, right]]
    got.append(hop(1, got[0]))
    left = pack_left(left_wide[0], left_narrow[0])
    mine, got, left = order.gate((), (mine, got, left))

    first = [0] + straight
    later = [m for m in range(1, chips) if m not in straight]
    for m in later:
        mine[m] = lax.ppermute(mine[0], "expert", [(i, i ^ (2 * m)) for i in range(experts)])
    for k in range(2, n - 1):
        got.append(hop(k, got[-1]))

    def sibling(piece):
        return lax.ppermute(piece, "expert", [(i, i ^ 1) for i in range(experts)])

    theirs_first = sibling(collect([mine[m] for m in first]))
    ends = [pair for pair in gather_pairs(1, 0) if pair in ((0, 1), (n - 1, n - 2))]
    others = [pair for pair in gather_pairs(1, 0) if pair not in ends]
    left_ends = lax.ppermute(left, "dp", ends)
    theirs_later = [sibling(mine[m]) for m in later]
    value = partial(first, later, [mine[m] for m in first + later], theirs_first, theirs_later)
    got, left, left_ends, value = order.gate((), (got, left, left_ends, value))

    one, two = chains
    sent, terms = {}, {}

    def hop_one(pairs, piece):
        return lax.ppermute(piece, "dp", pairs) if pairs else piece

    def make(chain, t):
        terms[chain.half, t] = product(chain, t, value, got)

    def wait(keys, more=(), values=()):
        ready, _, values = order.gate((), ([sent[key] for key in keys], more, values))
        sent.update(zip(keys, ready))
        return values

    def go(chain, t, s):
        term = terms[chain.half, t][s]
        if chain.adds(t, s):
            term = add(chain, t, s, term, sent[chain.half, t - 1, 1 - s])
        sent[chain.half, t, s] = lax.ppermute(term, "dp", chain.pairs(t, s))

    for k in range(max(2, n - 1), n):
        got.append(hop(k, got[-1]))
    for chain in chains:
        make(chain, 1)
        for s in chain.sets(1):
            go(chain, 1, s)
    left_odd = hop_one(gather_pairs(1, 1), left)
    inner = {target for _, target in ends}
    if all(pair[0] in inner for pair in gather_pairs(2, 1)):
        left_even = left_ends
    else:
        left_rest = hop_one(others, left)
        z = lax.axis_index("dp")
        left_even = jnp.where((z == 1) | (z == n - 2), left_ends, left_rest)
    second = [None, hop_one(gather_pairs(2, 1), left_even)]
    own = [product(chain, 0, value, got)[0] for chain in chains]

    got, value, left, left_odd = wait([(0, 1, s) for s in one.sets(1)], (), (got, value, left, left_odd))
    make(one, 2)
    if n == 4:
        go(one, 2, 0)
        go(one, 2, 1)
        left_rest = hop_one(others, left)
        make(two, 2)
        second[1], terms[1, 2] = wait([(1, 1, 0)], (), (second[1], terms[1, 2]))
        go(two, 2, 0)
        second[0] = hop_one(gather_pairs(2, 0), left_odd)
        make(one, 3)
        left_rest, terms[0, 3] = wait([(0, 2, 0)], (), (left_rest, terms[0, 3]))
        go(one, 3, 1)
        third = hop_one(gather_pairs(3, 0), second[1])
        terms[0, 3] = wait([(0, 2, 1)], (), terms[0, 3])
        go(one, 3, 0)
        make(two, 3)
        second[0], terms[1, 3], terms[1, 2] = wait([(1, 2, 0)], (), (second[0], terms[1, 3], terms[1, 2]))
        go(two, 3, 1)
        go(two, 2, 1)
        make(one, 4)
        terms[0, 4] = wait([(0, 3, 1)], (), terms[0, 4])
        go(one, 4, 0)
        third, terms[1, 3] = wait([], (), (third, terms[1, 3]))
        go(two, 3, 0)
        make(two, 4)
        terms[1, 4] = wait([(1, 3, 1), (0, 3, 0)], (), terms[1, 4])
        go(two, 4, 0)
        lefts = [[left, left], [left_even, left_odd], second, [third, third]]
    else:
        left_rest = hop_one(others, left)
        second[0] = hop_one(gather_pairs(2, 0), left_odd)
        lefts = [[left, left], [left_even, left_odd], second]
        for t in range(2, one.steps + 1):
            for chain in chains:
                if (chain.half, t) != (0, 2):
                    make(chain, t)
                before = [(chain.half, t - 1, s) for s in chain.sets(t - 1)]
                terms[chain.half, t] = wait(before, (), terms[chain.half, t])
                for s in chain.sets(t):
                    go(chain, t, s)
            if 2 < t < n:
                lefts.append(hop(t, wait([], (), lefts[-1])))

    left_inputs = [left, left_ends, left_rest, left_odd] + [item for pair in lefts[2:] for item in pair]
    left_w, left_n = pl.pallas_call(
        functools.partial(left_kernel, root, n),
        in_specs=[ANY] * len(left_inputs),
        out_shape=(
            jax.ShapeDtypeStruct((block, block), BF16),
            jax.ShapeDtypeStruct((rest, rest), BF16),
        ),
        scratch_shapes=[pltpu.VMEM((n,) + root.shape, BF16), pltpu.SemaphoreType.DMA((n,))],
        compiler_params=params(32),
        cost_estimate=cost(),
        name="left",
    )(*left_inputs)

    keys = sorted({(chain.half, t, s) for chain in chains for here in range(n) for t, s in chain.arrivals(here)})
    last = [(1, two.steps, s) for s in two.sets(two.steps)]
    early = [key for key in keys if key not in last]
    last = [key for key in keys if key in last]
    own = wait(early, (left_w, left_n), own)
    totals = pl.pallas_call(
        functools.partial(total_kernel, chains, early),
        in_specs=[VMEM] * (len(chains) + len(early)),
        out_specs=[VMEM] * len(chains),
        out_shape=[jax.ShapeDtypeStruct(chain.fold.shape, F32) for chain in chains],
        compiler_params=params(32),
        cost_estimate=cost(3),
        name="total",
    )(*own, *[sent[key] for key in early])
    out_w, out_n = pl.pallas_call(
        functools.partial(final_kernel, chains, block, last),
        in_specs=[VMEM] * (len(chains) + len(last) + 2),
        out_specs=[VMEM] * 2,
        out_shape=[jax.ShapeDtypeStruct((ffn, wide), F32), jax.ShapeDtypeStruct((ffn, narrow), F32)],
        scratch_shapes=[pltpu.VMEM(chain.fold.shape, BF16) for chain in chains],
        compiler_params=params(32),
        cost_estimate=cost(),
        name="final",
    )(*totals, *[sent[key] for key in last], left_w, left_n)
    return out_w[None], out_n[None]


def solution(mesh):
    return jax.shard_map(
        body,
        mesh=mesh,
        in_specs=(
            P(("dp", "expert"), None),
            P(("dp", "expert"), None),
            P(("dp", "expert"), None),
            P(("dp", "expert"), None),
            P("dp", "expert", None, None, None),
            P("expert", None, "dp"),
            P("expert", None, "dp"),
            P("expert", None, "dp"),
            P("expert", None, "dp"),
        ),
        out_specs=(P("expert", None, "dp"), P("expert", None, "dp")),
        check_vma=False,
    )
```

```python
import functools

import jax
import jax.numpy as jnp
from jax import lax
from jax.experimental import pallas as pl
from jax.experimental.pallas import tpu as pltpu
from jax.sharding import PartitionSpec as P

BF16 = jnp.bfloat16
F32 = jnp.float32
LANES = 128
META_ROWS = 16
ROW_CHUNKS = 3
MIB = 1024 * 1024


def round_up(value, unit):
    return (value + unit - 1) // unit * unit


def params(mib):
    return pltpu.CompilerParams(vmem_limit_bytes=mib * MIB)


def cost(micros=0):
    return pl.CostEstimate(flops=int(micros * 1.15e9), bytes_accessed=0, transcendentals=0)


class Order:
    def __init__(self, tick):
        self.tick = tick

    def gate(self, ready, values):
        self.tick, _, values = lax.optimization_barrier((self.tick, ready, values))
        return values


def dot_nn(left, right):
    return lax.dot_general(left, right, (((1,), (0,)), ((), ())), preferred_element_type=F32)


def dot_nt(left, right):
    return lax.dot_general(left, right, (((1,), (1,)), ((), ())), preferred_element_type=F32)


ANY = pl.BlockSpec(memory_space=pl.ANY)
VMEM = pl.BlockSpec(memory_space=pltpu.VMEM)


class Fold:
    def __init__(self, rows_w, rows_n, wide, narrow, tuck=False):
        self.rows_w, self.rows_n, self.wide, self.narrow = rows_w, rows_n, wide, narrow
        self.lanes = round_up(wide, LANES)
        self.step = round_up(narrow, LANES)
        self.ways = max(1, self.lanes // self.step)
        while rows_n % (self.ways * 16):
            self.ways -= 1
        self.tucked, self.group = 0, narrow
        if tuck:
            for rows in range(16, min(rows_w, rows_n) + 1, 16):
                group = -(-narrow // (rows_w // rows))
                if group <= self.lanes - wide and (rows_n - rows) % (self.ways * 16) == 0:
                    self.tucked, self.group = rows, group
        self.part = (rows_n - self.tucked) // self.ways
        self.rows = rows_w + self.part
        self.shape = (self.rows, self.lanes)

    def places(self):
        found = []
        if self.tucked:
            for i, start in enumerate(range(0, self.narrow, self.group)):
                stop = min(self.narrow, start + self.group)
                found.append(
                    (
                        slice(0, self.tucked),
                        slice(start, stop),
                        slice(i * self.tucked, (i + 1) * self.tucked),
                        slice(self.wide, self.wide + stop - start),
                    )
                )
        for way in range(self.ways if self.part else 0):
            low = self.tucked + way * self.part
            found.append(
                (
                    slice(low, low + self.part),
                    slice(0, self.narrow),
                    slice(self.rows_w, self.rows),
                    slice(way * self.step, way * self.step + self.narrow),
                )
            )
        return found

    def write(self, ref, wide_value, narrow_value):
        ref[...] = jnp.zeros(self.shape, ref.dtype)
        ref[0 : self.rows_w, 0 : self.wide] = wide_value
        for rows, columns, at_rows, at_lanes in self.places():
            ref[at_rows, at_lanes] = narrow_value[rows, columns]

    def wide_of(self, value):
        return value[0 : self.rows_w, 0 : self.wide]

    def narrow_of(self, value):
        parts = [value[at_rows, at_lanes] for _, _, at_rows, at_lanes in self.places()]
        return parts[0] if len(parts) == 1 else jnp.concatenate(parts, axis=0)

    def put_narrow(self, value, ref, low_row, low_column):
        for rows, columns, at_rows, at_lanes in self.places():
            ref[
                low_row + rows.start : low_row + rows.stop, low_column + columns.start : low_column + columns.stop
            ] = value[at_rows, at_lanes]


def token_kernel(root, cot_ref, gate_ref, route_ref, slot_ref, rw_ref, rn_ref, tok_ref, right_ref,
                 gate, route, slot, wide, narrow, meta, sem):
    width = cot_ref.shape[0]
    ways = gate_ref.shape[0]
    sources = (rw_ref, rn_ref, gate_ref, route_ref, slot_ref, cot_ref)
    targets = (wide, narrow, gate, route, slot, tok_ref.at[pl.ds(0, width)])
    copies = [
        pltpu.make_async_copy(source, target, sem.at[i])
        for i, (source, target) in enumerate(zip(sources, targets))
    ]
    for copy in copies:
        copy.start()
    for copy in copies[:5]:
        copy.wait()
    root.write(right_ref, wide[...], narrow[...])
    meta[...] = jnp.zeros(meta.shape, F32)
    meta[0:ways, :] = gate[...].astype(F32)
    meta[ways : 2 * ways, :] = route[...].astype(F32)
    meta[2 * ways : 3 * ways, :] = slot[...].astype(F32)
    tok_ref[width : width + META_ROWS, :] = meta[...].astype(BF16)
    copies[5].wait()


def pack_left_kernel(root, lw_ref, ln_ref, out_ref, wide, narrow, sem):
    copies = [
        pltpu.make_async_copy(lw_ref, wide, sem.at[0]),
        pltpu.make_async_copy(ln_ref, narrow, sem.at[1]),
    ]
    for copy in copies:
        copy.start()
    for copy in copies:
        copy.wait()
    root.write(out_ref, wide[...], narrow[...])


def partial_kernel(topk, width, block, gap, first, later, hidden_ref, *refs):
    sources, _, capacity = hidden_ref.shape
    out_ref, rows_ref = refs[-2:]
    token_refs = {}
    for i, m in enumerate(first + later):
        token_refs[2 * m] = refs[i]
        if i < len(first):
            token_refs[2 * m + 1] = refs[len(first + later)].at[i]
        else:
            token_refs[2 * m + 1] = refs[len(first + later) + 1 + i - len(first)]
    expert = lax.axis_index("expert")
    parts = ((0, block, 0), (block, width, gap))

    @pl.when(pl.program_id(0) == 0)
    def _():
        for offset in range(sources):
            token_ref = token_refs[offset]
            source = jnp.bitwise_xor(expert, offset)
            meta = token_ref[width : width + META_ROWS, :].astype(F32)
            tokens = meta.shape[1]
            place = lax.broadcasted_iota(jnp.int32, (capacity, tokens), 0).astype(F32)
            here = expert.astype(F32)
            weights = jnp.zeros((capacity, tokens), F32)
            for k in range(topk):
                gate = meta[k : k + 1, :]
                route = meta[topk + k : topk + k + 1, :]
                slot = meta[2 * topk + k : 2 * topk + k + 1, :]
                wanted = jnp.where(route == here, slot, -1.0)
                weights = jnp.where(place == wanted, gate, weights)
            weights = weights.astype(BF16)
            rows = pl.ds(pl.multiple_of(source * capacity, capacity), capacity)
            for low, high, at in parts:
                value = dot_nt(weights, token_ref[low:high, :]).astype(BF16)
                rows_ref[rows, at : at + high - low] = value

    if capacity % LANES == 0:
        hidden = jnp.concatenate([hidden_ref[s] for s in range(sources)], axis=1)
    for low, high, at in parts:
        columns = slice(at, at + high - low)
        if capacity % LANES == 0:
            total = dot_nn(hidden, rows_ref[:, columns])
        else:
            total = dot_nn(hidden_ref[0], rows_ref[0:capacity, columns])
            for s in range(1, sources):
                total += dot_nn(hidden_ref[s], rows_ref[s * capacity : (s + 1) * capacity, columns])
        out_ref[:, columns] = total.astype(BF16)


class Chain:
    def __init__(self, n, half, order, low, fold):
        self.n, self.half, self.order, self.low, self.fold = n, half, order, low, fold
        self.steps = max(t for t in range(1, 2 * n) if self.pairs(t, 0) or self.pairs(t, 1))

    def distance(self, t, z, s):
        i = z if z % 2 == s else self.n - 1 - z
        if (z % 2 == s and z == self.n - 1) or (z % 2 != s and z == 0):
            return 0
        k = t - 1 - i
        if 0 <= k < len(self.order) and self.order[k] > i:
            return self.order[k] - i
        return 0

    def pairs(self, t, s):
        return [
            (z, z + 1 if z % 2 == s else z - 1) for z in range(self.n) if self.distance(t, z, s)
        ]

    def sets(self, t):
        return [s for s in (0, 1) if self.pairs(t, s)]

    def adds(self, t, s):
        targets = {target for _, target in self.pairs(t - 1, 1 - s)} if t > 1 else set()
        return any(z in targets for z, _ in self.pairs(t, s))

    def arrivals(self, z):
        found = []
        for t in range(1, self.steps + 1):
            for s in (0, 1):
                for sender, target in self.pairs(t, s):
                    if target == z and self.distance(t, sender, s) == 1:
                        found.append((t, s))
        return found


def product_kernel(chain, t, keys, root, block, gap, partial_ref, *refs):
    root_refs = dict(zip(keys, refs))
    out_refs, piece_ref = refs[len(keys) : -1], refs[-1]
    z = lax.axis_index("dp")
    fold = chain.fold

    def product(root_ref, out_ref):
        piece = root_ref[...]
        rows = slice(chain.low, chain.low + fold.rows_w)
        wide = dot_nn(partial_ref[rows, 0:block], root.wide_of(piece))
        narrow = dot_nn(partial_ref[rows, gap : gap + root.rows_n], root.narrow_of(piece))
        fold.write(out_ref, wide.astype(BF16), narrow.astype(BF16))

    def take(root_ref):
        piece_ref[...] = root_ref[...]

    if t == 0:
        product(root_refs[0, 0], out_refs[0])
        return
    for s, out_ref in zip(chain.sets(t), out_refs):
        by_far = {}
        for here in range(chain.n):
            far = chain.distance(t, here, s)
            if far:
                by_far[far] = by_far.get(far, False) | (z == here)
        if len(by_far) <= 2:
            for far, here in by_far.items():
                pl.when(here)(functools.partial(product, root_refs[far, s], out_ref))
        else:
            for far, here in by_far.items():
                pl.when(here)(functools.partial(take, root_refs[far, s]))
            here = functools.reduce(jnp.logical_or, by_far.values())
            pl.when(here)(functools.partial(product, piece_ref, out_ref))


def add_kernel(chain, t, s, term_ref, got_ref, out_ref):
    z = lax.axis_index("dp")
    sends = functools.reduce(jnp.logical_or, [z == here for here, _ in chain.pairs(t, s)])

    @pl.when(sends)
    def _():
        out_ref[...] = (term_ref[...].astype(F32) + got_ref[...].astype(F32)).astype(BF16)


def left_kernel(root, n, own_ref, ends_ref, rest_ref, odd_ref, *refs):
    got = refs[: 2 * (n - 2)]
    wide_ref, narrow_ref, held, sem = refs[2 * (n - 2) :]
    z = lax.axis_index("dp")
    for here in range(n):
        even_ref = ends_ref if here in (1, n - 2) else rest_ref
        near = (even_ref, odd_ref) + got

        @pl.when(z == here)
        def _():
            copies = [pltpu.make_async_copy(own_ref, held.at[here], sem.at[here])]
            for q in range(n):
                if q != here:
                    s = here % 2 if q > here else 1 - here % 2
                    copies.append(
                        pltpu.make_async_copy(near[2 * (abs(q - here) - 1) + s], held.at[q], sem.at[q])
                    )
            for copy in copies:
                copy.start()
            for copy in copies:
                copy.wait()

    for q in range(n):
        piece = held[q]
        wide_ref[:, q * root.wide : (q + 1) * root.wide] = root.wide_of(piece)
        root.put_narrow(piece, narrow_ref, 0, q * root.narrow)


def add_arrivals(chains, got_refs, own_refs, out_refs, dtype):
    z = lax.axis_index("dp")
    for here in range(chains[0].n):

        @pl.when(z == here)
        def _():
            for chain, own_ref, out_ref in zip(chains, own_refs, out_refs):
                value = own_ref[...].astype(F32)
                for t, s in chain.arrivals(here):
                    if (chain.half, t, s) in got_refs:
                        value += got_refs[chain.half, t, s][...].astype(F32)
                out_ref[...] = value.astype(dtype)


def total_kernel(chains, keys, *refs):
    got_refs = dict(zip(keys, refs[len(chains) :]))
    add_arrivals(chains, got_refs, refs[: len(chains)], refs[len(chains) + len(keys) :], F32)


def final_kernel(chains, block, keys, *refs):
    got_refs = dict(zip(keys, refs[len(chains) :]))
    wide_ref, narrow_ref, out_w_ref, out_n_ref = refs[len(chains) + len(keys) :][:4]
    totals, narrow_rows = refs[len(refs) - len(chains) - 1 : -1], refs[-1]
    add_arrivals(chains, got_refs, refs[: len(chains)], totals, BF16)
    values = [total[...] for total in totals]
    for chain, value in zip(chains, values):
        chain.fold.put_narrow(value, narrow_rows, chain.low, 0)
    wide_rows = jnp.concatenate([chain.fold.wide_of(value) for chain, value in zip(chains, values)], axis=0)
    for rows, out_ref in ((wide_rows, out_w_ref), (narrow_rows[...], out_n_ref)):
        out_ref[0:block, :] = dot_nn(wide_ref[...], rows[0:block])
        out_ref[block:, :] = dot_nn(narrow_ref[...], rows[block:])


def collect_kernel(count, *refs):
    sem = refs[-1]
    out_ref = refs[count]
    copies = [pltpu.make_async_copy(refs[i], out_ref.at[i], sem.at[i]) for i in range(count)]
    for copy in copies:
        copy.start()
    for copy in copies:
        copy.wait()


def body(
    cotangent, gates, routes, slots, saved_hidden, left_wide, left_narrow, right_wide, right_narrow
):
    tokens, width = cotangent.shape
    topk = gates.shape[1]
    n = lax.axis_size("dp")
    experts = lax.axis_size("expert")
    chips = experts // 2
    _, _, sources, capacity, ffn = saved_hidden.shape
    block, wide = right_wide.shape[1:]
    rest, narrow = right_narrow.shape[1:]
    gap = round_up(block, LANES)
    span = gap + round_up(rest, LANES)
    root = Fold(block, rest, wide, narrow)
    left_root = Fold(block, rest, wide, narrow, True)
    cut = ffn // 64 * 32
    folds = [Fold(rows, rows, wide, narrow, True) for rows in (cut, ffn - cut)]
    sooner = [n - 2, n - 1] if n > 2 else [1]
    chains = [
        Chain(n, 0, sooner + list(range(n - 3, 0, -1)), 0, folds[0]),
        Chain(n, 1, list(range(n - 1, 0, -1)), cut, folds[1]),
    ]

    def gather_pairs(k, s):
        up = [(i, i + 1) for i in range(s, n - 1, 2) if i >= k - 1]
        return up + [(i + 1, i) for i in range(s, n - 1, 2) if i <= n - 1 - k]

    def hop(k, pieces):
        return [
            lax.ppermute(pieces[1 - s], "dp", gather_pairs(k, s)) if gather_pairs(k, s) else pieces[1 - s]
            for s in (0, 1)
        ]

    tok, right = pl.pallas_call(
        functools.partial(token_kernel, root),
        in_specs=[ANY] * 6,
        out_specs=[VMEM] * 2,
        out_shape=[
            jax.ShapeDtypeStruct((width + META_ROWS, tokens), BF16),
            jax.ShapeDtypeStruct(root.shape, BF16),
        ],
        scratch_shapes=[
            pltpu.VMEM((topk, tokens), BF16),
            pltpu.VMEM((topk, tokens), jnp.int32),
            pltpu.VMEM((topk, tokens), jnp.int32),
            pltpu.VMEM((block, wide), BF16),
            pltpu.VMEM((rest, narrow), BF16),
            pltpu.VMEM((META_ROWS, tokens), F32),
            pltpu.SemaphoreType.DMA((6,)),
        ],
        compiler_params=params(56),
        cost_estimate=cost(),
        name="tokens",
    )(cotangent.T, gates.T, routes.T, slots.T, right_wide[0], right_narrow[0])

    def collect(values):
        count = len(values)
        return pl.pallas_call(
            functools.partial(collect_kernel, count),
            in_specs=[ANY] * count,
            out_specs=ANY,
            out_shape=jax.ShapeDtypeStruct((count,) + tok.shape, BF16),
            scratch_shapes=[pltpu.SemaphoreType.DMA((count,))],
            compiler_params=params(16),
            cost_estimate=cost(),
            name="collect",
        )(*values)

    def pack_left(wide_piece, narrow_piece):
        return pl.pallas_call(
            functools.partial(pack_left_kernel, left_root),
            in_specs=[ANY] * 2,
            out_shape=jax.ShapeDtypeStruct(left_root.shape, BF16),
            scratch_shapes=[
                pltpu.VMEM((block, wide), BF16),
                pltpu.VMEM((rest, narrow), BF16),
                pltpu.SemaphoreType.DMA((2,)),
            ],
            compiler_params=params(16),
            cost_estimate=cost(),
            name="pack_left",
        )(wide_piece, narrow_piece)

    chunk_rows = ffn // ROW_CHUNKS
    hidden = jnp.swapaxes(saved_hidden[0, 0], 1, 2)

    def partial(first, later, mine, theirs_first, theirs_later):
        return pl.pallas_call(
            functools.partial(partial_kernel, topk, width, block, gap, first, later),
            grid=(ROW_CHUNKS,),
            in_specs=[pl.BlockSpec((sources, chunk_rows, capacity), lambda i: (0, i, 0))]
            + [VMEM] * (1 + len(mine) + len(later)),
            out_specs=pl.BlockSpec((chunk_rows, span), lambda i: (i, 0)),
            out_shape=jax.ShapeDtypeStruct((ffn, span), BF16),
            scratch_shapes=[pltpu.VMEM((sources * capacity, span), BF16)],
            compiler_params=params(32),
            cost_estimate=cost(),
            name="partial",
        )(hidden, *mine, theirs_first, *theirs_later)

    def product(chain, t, value, got):
        keys = [(0, 0)]
        if t:
            keys = sorted({(chain.distance(t, z, s), s) for z in range(n) for s in (0, 1)})
            keys = [key for key in keys if key[0]]
        sets = chain.sets(t) if t else [0]
        made = pl.pallas_call(
            functools.partial(product_kernel, chain, t, keys, root, block, gap),
            in_specs=[VMEM] * (1 + len(keys)),
            out_specs=[VMEM] * len(sets),
            out_shape=[jax.ShapeDtypeStruct(chain.fold.shape, BF16)] * len(sets),
            scratch_shapes=[pltpu.VMEM(root.shape, BF16)],
            compiler_params=params(16),
            cost_estimate=cost(),
            name="product",
        )(value, *[got[far][s] for far, s in keys])
        return dict(zip(sets, made))

    def add(chain, t, s, term, got):
        return pl.pallas_call(
            functools.partial(add_kernel, chain, t, s),
            in_specs=[VMEM] * 2,
            out_specs=VMEM,
            out_shape=jax.ShapeDtypeStruct(term.shape, BF16),
            compiler_params=params(16),
            cost_estimate=cost(),
            name="add",
        )(term, got)

    order = Order(slots)
    straight = [m for m in range(1, chips) if m & (m - 1) == 0]
    mine = {0: tok}
    for m in straight:
        mine[m] = lax.ppermute(tok, "expert", [(i, i ^ (2 * m)) for i in range(experts)])
    got = [[right, right]]
    got.append(hop(1, got[0]))
    left = pack_left(left_wide[0], left_narrow[0])
    mine, got, left = order.gate((), (mine, got, left))

    first = [0] + straight
    later = [m for m in range(1, chips) if m not in straight]
    for m in later:
        mine[m] = lax.ppermute(mine[0], "expert", [(i, i ^ (2 * m)) for i in range(experts)])
    for k in range(2, n - 1):
        got.append(hop(k, got[-1]))

    def sibling(piece):
        return lax.ppermute(piece, "expert", [(i, i ^ 1) for i in range(experts)])

    theirs_first = sibling(collect([mine[m] for m in first]))
    ends = [pair for pair in gather_pairs(1, 0) if pair in ((0, 1), (n - 1, n - 2))]
    others = [pair for pair in gather_pairs(1, 0) if pair not in ends]
    left_ends = lax.ppermute(left, "dp", ends)
    theirs_later = [sibling(mine[m]) for m in later]
    value = partial(first, later, [mine[m] for m in first + later], theirs_first, theirs_later)
    got, left, left_ends, value = order.gate((), (got, left, left_ends, value))

    one, two = chains
    sent, terms = {}, {}

    def hop_one(pairs, piece):
        return lax.ppermute(piece, "dp", pairs) if pairs else piece

    def make(chain, t):
        terms[chain.half, t] = product(chain, t, value, got)

    def wait(keys, more=(), values=()):
        ready, _, values = order.gate((), ([sent[key] for key in keys], more, values))
        sent.update(zip(keys, ready))
        return values

    def go(chain, t, s):
        term = terms[chain.half, t][s]
        if chain.adds(t, s):
            term = add(chain, t, s, term, sent[chain.half, t - 1, 1 - s])
        sent[chain.half, t, s] = lax.ppermute(term, "dp", chain.pairs(t, s))

    make(one, 1)
    for s in one.sets(1):
        go(one, 1, s)
    for k in range(max(2, n - 1), n):
        got.append(hop(k, got[-1]))
    left_odd = hop_one(gather_pairs(1, 1), left)
    left_rest = hop_one(others, left)
    inner = {target for _, target in ends}
    if all(pair[0] in inner for pair in gather_pairs(2, 1)):
        left_even = left_ends
    else:
        z = lax.axis_index("dp")
        left_even = jnp.where((z == 1) | (z == n - 2), left_ends, left_rest)
    second = [None, hop_one(gather_pairs(2, 1), left_even)]
    own = [product(chain, 0, value, got)[0] for chain in chains]

    got, value, left_odd = wait([(0, 1, s) for s in one.sets(1)], (), (got, value, left_odd))
    make(two, 1)
    make(one, 2)
    for s in two.sets(1):
        go(two, 1, s)
    if n == 4:
        go(one, 2, 1)
        second[0] = hop_one(gather_pairs(2, 0), left_odd)
        left_rest, second[1], terms[0, 2] = wait([], (), (left_rest, second[1], terms[0, 2]))
        go(one, 2, 0)
        third = hop_one(gather_pairs(3, 0), second[1])
        make(two, 2)
        second[0], terms[1, 2] = wait([(1, 1, 0)], (), (second[0], terms[1, 2]))
        go(two, 2, 1)
        go(two, 2, 0)
        make(one, 3)
        terms[0, 3] = wait([(0, 2, 0), (0, 2, 1)], (), terms[0, 3])
        go(one, 3, 1)
        go(one, 3, 0)
        make(two, 3)
        third, terms[1, 3] = wait([(1, 2, 1)], (), (third, terms[1, 3]))
        go(two, 3, 0)
        make(one, 4)
        terms[0, 4], terms[1, 3] = wait([(0, 3, 1), (1, 2, 0)], (), (terms[0, 4], terms[1, 3]))
        go(one, 4, 0)
        go(two, 3, 1)
        lefts = [[left, left], [left_even, left_odd], second, [third, third]]
    else:
        for s in one.sets(2):
            go(one, 2, s)
        second[0] = hop_one(gather_pairs(2, 0), left_odd)
        lefts = [[left, left], [left_even, left_odd], second]
        for t in range(2, max(chain.steps for chain in chains) + 1):
            for chain in chains:
                if t <= chain.steps and (chain.half, t) != (0, 2):
                    make(chain, t)
                    before = [(chain.half, t - 1, s) for s in chain.sets(t - 1)]
                    terms[chain.half, t] = wait(before, (), terms[chain.half, t])
                    for s in chain.sets(t):
                        go(chain, t, s)
            if 2 < t < n:
                lefts.append(hop(t, wait([], (), lefts[-1])))

    left_inputs = [left, left_ends, left_rest, left_odd] + [item for pair in lefts[2:] for item in pair]
    left_w, left_n = pl.pallas_call(
        functools.partial(left_kernel, left_root, n),
        in_specs=[ANY] * len(left_inputs),
        out_shape=(
            jax.ShapeDtypeStruct((block, block), BF16),
            jax.ShapeDtypeStruct((rest, rest), BF16),
        ),
        scratch_shapes=[pltpu.VMEM((n,) + left_root.shape, BF16), pltpu.SemaphoreType.DMA((n,))],
        compiler_params=params(32),
        cost_estimate=cost(),
        name="left",
    )(*left_inputs)

    keys = sorted({(chain.half, t, s) for chain in chains for here in range(n) for t, s in chain.arrivals(here)})
    last = [(0, one.steps, s) for s in one.sets(one.steps)] + [(1, two.steps, 1)]
    early = [key for key in keys if key not in last]
    last = [key for key in keys if key in last]
    own = wait(early, (left_w, left_n), own)
    totals = pl.pallas_call(
        functools.partial(total_kernel, chains, early),
        in_specs=[VMEM] * (len(chains) + len(early)),
        out_specs=[VMEM] * len(chains),
        out_shape=[jax.ShapeDtypeStruct(chain.fold.shape, F32) for chain in chains],
        compiler_params=params(32),
        cost_estimate=cost(3),
        name="total",
    )(*own, *[sent[key] for key in early])
    out_w, out_n = pl.pallas_call(
        functools.partial(final_kernel, chains, block, last),
        in_specs=[VMEM] * (len(chains) + len(last) + 2),
        out_specs=[VMEM] * 2,
        out_shape=[jax.ShapeDtypeStruct((ffn, wide), F32), jax.ShapeDtypeStruct((ffn, narrow), F32)],
        scratch_shapes=[pltpu.VMEM(chain.fold.shape, BF16) for chain in chains]
        + [pltpu.VMEM((ffn, narrow), BF16)],
        compiler_params=params(32),
        cost_estimate=cost(),
        name="final",
    )(*totals, *[sent[key] for key in last], left_w, left_n)
    return out_w[None], out_n[None]


def solution(mesh):
    return jax.shard_map(
        body,
        mesh=mesh,
        in_specs=(
            P(("dp", "expert"), None),
            P(("dp", "expert"), None),
            P(("dp", "expert"), None),
            P(("dp", "expert"), None),
            P("dp", "expert", None, None, None),
            P("expert", None, "dp"),
            P("expert", None, "dp"),
            P("expert", None, "dp"),
            P("expert", None, "dp"),
        ),
        out_specs=(P("expert", None, "dp"), P("expert", None, "dp")),
        check_vma=False,
    )
```

```python
import functools

import jax
import jax.numpy as jnp
from jax import lax
from jax.experimental import pallas as pl
from jax.experimental.pallas import tpu as pltpu
from jax.sharding import PartitionSpec as P

BF16 = jnp.bfloat16
F32 = jnp.float32
LANES = 128
META_ROWS = 16
ROW_CHUNKS = 3
MIB = 1024 * 1024


def round_up(value, unit):
    return (value + unit - 1) // unit * unit


def params(mib):
    return pltpu.CompilerParams(vmem_limit_bytes=mib * MIB)


def cost(micros=0):
    return pl.CostEstimate(flops=int(micros * 1.15e9), bytes_accessed=0, transcendentals=0)


class Order:
    def __init__(self, tick):
        self.tick = tick

    def gate(self, ready, values):
        self.tick, _, values = lax.optimization_barrier((self.tick, ready, values))
        return values


def dot_nn(left, right):
    return lax.dot_general(left, right, (((1,), (0,)), ((), ())), preferred_element_type=F32)


def dot_nt(left, right):
    return lax.dot_general(left, right, (((1,), (1,)), ((), ())), preferred_element_type=F32)


ANY = pl.BlockSpec(memory_space=pl.ANY)
VMEM = pl.BlockSpec(memory_space=pltpu.VMEM)


class Fold:
    def __init__(self, rows_w, rows_n, wide, narrow, tuck=False):
        self.rows_w, self.rows_n, self.wide, self.narrow = rows_w, rows_n, wide, narrow
        self.lanes = round_up(wide, LANES)
        self.step = round_up(narrow, LANES)
        self.ways = max(1, self.lanes // self.step)
        while rows_n % (self.ways * 16):
            self.ways -= 1
        self.tucked, self.group = 0, narrow
        if tuck:
            for rows in range(16, min(rows_w, rows_n) + 1, 16):
                group = -(-narrow // (rows_w // rows))
                if group <= self.lanes - wide and (rows_n - rows) % (self.ways * 16) == 0:
                    self.tucked, self.group = rows, group
        self.part = (rows_n - self.tucked) // self.ways
        self.rows = rows_w + self.part
        self.shape = (self.rows, self.lanes)

    def places(self):
        found = []
        if self.tucked:
            for i, start in enumerate(range(0, self.narrow, self.group)):
                stop = min(self.narrow, start + self.group)
                found.append(
                    (
                        slice(0, self.tucked),
                        slice(start, stop),
                        slice(i * self.tucked, (i + 1) * self.tucked),
                        slice(self.wide, self.wide + stop - start),
                    )
                )
        for way in range(self.ways if self.part else 0):
            low = self.tucked + way * self.part
            found.append(
                (
                    slice(low, low + self.part),
                    slice(0, self.narrow),
                    slice(self.rows_w, self.rows),
                    slice(way * self.step, way * self.step + self.narrow),
                )
            )
        return found

    def write(self, ref, wide_value, narrow_value):
        ref[...] = jnp.zeros(self.shape, ref.dtype)
        ref[0 : self.rows_w, 0 : self.wide] = wide_value
        for rows, columns, at_rows, at_lanes in self.places():
            ref[at_rows, at_lanes] = narrow_value[rows, columns]

    def wide_of(self, value):
        return value[0 : self.rows_w, 0 : self.wide]

    def narrow_of(self, value):
        parts = [value[at_rows, at_lanes] for _, _, at_rows, at_lanes in self.places()]
        return parts[0] if len(parts) == 1 else jnp.concatenate(parts, axis=0)

    def put_narrow(self, value, ref, low_row, low_column):
        for rows, columns, at_rows, at_lanes in self.places():
            ref[
                low_row + rows.start : low_row + rows.stop, low_column + columns.start : low_column + columns.stop
            ] = value[at_rows, at_lanes]


def token_kernel(root, cot_ref, gate_ref, route_ref, slot_ref, rw_ref, rn_ref, tok_ref, right_ref,
                 gate, route, slot, wide, narrow, meta, sem):
    width = cot_ref.shape[0]
    ways = gate_ref.shape[0]
    sources = (rw_ref, rn_ref, gate_ref, route_ref, slot_ref, cot_ref)
    targets = (wide, narrow, gate, route, slot, tok_ref.at[pl.ds(0, width)])
    copies = [
        pltpu.make_async_copy(source, target, sem.at[i])
        for i, (source, target) in enumerate(zip(sources, targets))
    ]
    for copy in copies:
        copy.start()
    for copy in copies[:5]:
        copy.wait()
    root.write(right_ref, wide[...], narrow[...])
    meta[...] = jnp.zeros(meta.shape, F32)
    meta[0:ways, :] = gate[...].astype(F32)
    meta[ways : 2 * ways, :] = route[...].astype(F32)
    meta[2 * ways : 3 * ways, :] = slot[...].astype(F32)
    tok_ref[width : width + META_ROWS, :] = meta[...].astype(BF16)
    copies[5].wait()


def pack_left_kernel(root, lw_ref, ln_ref, out_ref, wide, narrow, sem):
    copies = [
        pltpu.make_async_copy(lw_ref, wide, sem.at[0]),
        pltpu.make_async_copy(ln_ref, narrow, sem.at[1]),
    ]
    for copy in copies:
        copy.start()
    for copy in copies:
        copy.wait()
    root.write(out_ref, wide[...], narrow[...])


def partial_kernel(topk, width, block, gap, first, later, hidden_ref, *refs):
    sources, _, capacity = hidden_ref.shape
    out_ref, rows_ref = refs[-2:]
    token_refs = {}
    for i, m in enumerate(first + later):
        token_refs[2 * m] = refs[i]
        if i < len(first):
            token_refs[2 * m + 1] = refs[len(first + later)].at[i]
        else:
            token_refs[2 * m + 1] = refs[len(first + later) + 1 + i - len(first)]
    expert = lax.axis_index("expert")
    parts = ((0, block, 0), (block, width, gap))

    @pl.when(pl.program_id(0) == 0)
    def _():
        for offset in range(sources):
            token_ref = token_refs[offset]
            source = jnp.bitwise_xor(expert, offset)
            meta = token_ref[width : width + META_ROWS, :].astype(F32)
            tokens = meta.shape[1]
            place = lax.broadcasted_iota(jnp.int32, (capacity, tokens), 0).astype(F32)
            here = expert.astype(F32)
            weights = jnp.zeros((capacity, tokens), F32)
            for k in range(topk):
                gate = meta[k : k + 1, :]
                route = meta[topk + k : topk + k + 1, :]
                slot = meta[2 * topk + k : 2 * topk + k + 1, :]
                wanted = jnp.where(route == here, slot, -1.0)
                weights = jnp.where(place == wanted, gate, weights)
            weights = weights.astype(BF16)
            rows = pl.ds(pl.multiple_of(source * capacity, capacity), capacity)
            for low, high, at in parts:
                value = dot_nt(weights, token_ref[low:high, :]).astype(BF16)
                rows_ref[rows, at : at + high - low] = value

    if capacity % LANES == 0:
        hidden = jnp.concatenate([hidden_ref[s] for s in range(sources)], axis=1)
    for low, high, at in parts:
        columns = slice(at, at + high - low)
        if capacity % LANES == 0:
            total = dot_nn(hidden, rows_ref[:, columns])
        else:
            total = dot_nn(hidden_ref[0], rows_ref[0:capacity, columns])
            for s in range(1, sources):
                total += dot_nn(hidden_ref[s], rows_ref[s * capacity : (s + 1) * capacity, columns])
        out_ref[:, columns] = total.astype(BF16)


class Chain:
    def __init__(self, n, half, order, low, fold):
        self.n, self.half, self.order, self.low, self.fold = n, half, order, low, fold
        self.steps = max(t for t in range(1, 2 * n) if self.pairs(t, 0) or self.pairs(t, 1))

    def distance(self, t, z, s):
        i = z if z % 2 == s else self.n - 1 - z
        if (z % 2 == s and z == self.n - 1) or (z % 2 != s and z == 0):
            return 0
        k = t - 1 - i
        if 0 <= k < len(self.order) and self.order[k] > i:
            return self.order[k] - i
        return 0

    def pairs(self, t, s):
        return [
            (z, z + 1 if z % 2 == s else z - 1) for z in range(self.n) if self.distance(t, z, s)
        ]

    def sets(self, t):
        return [s for s in (0, 1) if self.pairs(t, s)]

    def adds(self, t, s):
        targets = {target for _, target in self.pairs(t - 1, 1 - s)} if t > 1 else set()
        return any(z in targets for z, _ in self.pairs(t, s))

    def arrivals(self, z):
        found = []
        for t in range(1, self.steps + 1):
            for s in (0, 1):
                for sender, target in self.pairs(t, s):
                    if target == z and self.distance(t, sender, s) == 1:
                        found.append((t, s))
        return found


def product_kernel(chain, t, keys, root, block, gap, partial_ref, *refs):
    root_refs = dict(zip(keys, refs))
    out_refs, piece_ref = refs[len(keys) : -1], refs[-1]
    z = lax.axis_index("dp")
    fold = chain.fold

    def product(root_ref, out_ref):
        piece = root_ref[...]
        rows = slice(chain.low, chain.low + fold.rows_w)
        wide = dot_nn(partial_ref[rows, 0:block], root.wide_of(piece))
        narrow = dot_nn(partial_ref[rows, gap : gap + root.rows_n], root.narrow_of(piece))
        fold.write(out_ref, wide.astype(BF16), narrow.astype(BF16))

    def take(root_ref):
        piece_ref[...] = root_ref[...]

    if t == 0:
        product(root_refs[0, 0], out_refs[0])
        return
    for s, out_ref in zip(chain.sets(t), out_refs):
        by_far = {}
        for here in range(chain.n):
            far = chain.distance(t, here, s)
            if far:
                by_far[far] = by_far.get(far, False) | (z == here)
        if len(by_far) <= 2:
            for far, here in by_far.items():
                pl.when(here)(functools.partial(product, root_refs[far, s], out_ref))
        else:
            for far, here in by_far.items():
                pl.when(here)(functools.partial(take, root_refs[far, s]))
            here = functools.reduce(jnp.logical_or, by_far.values())
            pl.when(here)(functools.partial(product, piece_ref, out_ref))


def add_kernel(chain, t, s, term_ref, got_ref, out_ref):
    z = lax.axis_index("dp")
    sends = functools.reduce(jnp.logical_or, [z == here for here, _ in chain.pairs(t, s)])

    @pl.when(sends)
    def _():
        out_ref[...] = (term_ref[...].astype(F32) + got_ref[...].astype(F32)).astype(BF16)


def left_kernel(root, n, own_ref, ends_ref, rest_ref, odd_ref, *refs):
    got = refs[: 2 * (n - 2)]
    wide_ref, narrow_ref, held, sem = refs[2 * (n - 2) :]
    z = lax.axis_index("dp")
    for here in range(n):
        even_ref = ends_ref if here in (1, n - 2) else rest_ref
        near = (even_ref, odd_ref) + got

        @pl.when(z == here)
        def _():
            copies = [pltpu.make_async_copy(own_ref, held.at[here], sem.at[here])]
            for q in range(n):
                if q != here:
                    s = here % 2 if q > here else 1 - here % 2
                    copies.append(
                        pltpu.make_async_copy(near[2 * (abs(q - here) - 1) + s], held.at[q], sem.at[q])
                    )
            for copy in copies:
                copy.start()
            for copy in copies:
                copy.wait()

    for q in range(n):
        piece = held[q]
        wide_ref[:, q * root.wide : (q + 1) * root.wide] = root.wide_of(piece)
        root.put_narrow(piece, narrow_ref, 0, q * root.narrow)


def add_arrivals(chains, got_refs, own_refs, out_refs, dtype):
    z = lax.axis_index("dp")
    for here in range(chains[0].n):

        @pl.when(z == here)
        def _():
            for chain, own_ref, out_ref in zip(chains, own_refs, out_refs):
                value = own_ref[...].astype(F32)
                for t, s in chain.arrivals(here):
                    if (chain.half, t, s) in got_refs:
                        value += got_refs[chain.half, t, s][...].astype(F32)
                out_ref[...] = value.astype(dtype)


def total_kernel(chains, keys, order_ref, *refs):
    got_refs = dict(zip(keys, refs[len(chains) :]))
    add_arrivals(chains, got_refs, refs[: len(chains)], refs[len(chains) + len(keys) :], F32)


def final_kernel(chains, block, keys, *refs):
    got_refs = dict(zip(keys, refs[len(chains) :]))
    wide_ref, narrow_ref, out_w_ref, out_n_ref = refs[len(chains) + len(keys) :][:4]
    totals, narrow_rows = refs[len(refs) - len(chains) - 1 : -1], refs[-1]
    add_arrivals(chains, got_refs, refs[: len(chains)], totals, BF16)
    values = [total[...] for total in totals]
    for chain, value in zip(chains, values):
        chain.fold.put_narrow(value, narrow_rows, chain.low, 0)
    wide_rows = jnp.concatenate([chain.fold.wide_of(value) for chain, value in zip(chains, values)], axis=0)
    for rows, out_ref in ((wide_rows, out_w_ref), (narrow_rows[...], out_n_ref)):
        out_ref[0:block, :] = dot_nn(wide_ref[...], rows[0:block])
        out_ref[block:, :] = dot_nn(narrow_ref[...], rows[block:])


def collect_kernel(count, *refs):
    sem = refs[-1]
    out_ref = refs[count]
    copies = [pltpu.make_async_copy(refs[i], out_ref.at[i], sem.at[i]) for i in range(count)]
    for copy in copies:
        copy.start()
    for copy in copies:
        copy.wait()


def body(
    cotangent, gates, routes, slots, saved_hidden, left_wide, left_narrow, right_wide, right_narrow
):
    tokens, width = cotangent.shape
    topk = gates.shape[1]
    n = lax.axis_size("dp")
    experts = lax.axis_size("expert")
    chips = experts // 2
    _, _, sources, capacity, ffn = saved_hidden.shape
    block, wide = right_wide.shape[1:]
    rest, narrow = right_narrow.shape[1:]
    gap = round_up(block, LANES)
    span = gap + round_up(rest, LANES)
    root = Fold(block, rest, wide, narrow)
    left_root = Fold(block, rest, wide, narrow, True)
    cut = ffn // 64 * 32
    folds = [Fold(rows, rows, wide, narrow, True) for rows in (cut, ffn - cut)]
    sooner = [n - 2, n - 1] if n > 2 else [1]
    chains = [
        Chain(n, 0, sooner + list(range(n - 3, 0, -1)), 0, folds[0]),
        Chain(n, 1, list(range(n - 1, 0, -1)), cut, folds[1]),
    ]

    def gather_pairs(k, s):
        up = [(i, i + 1) for i in range(s, n - 1, 2) if i >= k - 1]
        return up + [(i + 1, i) for i in range(s, n - 1, 2) if i <= n - 1 - k]

    def hop(k, pieces):
        return [
            lax.ppermute(pieces[1 - s], "dp", gather_pairs(k, s)) if gather_pairs(k, s) else pieces[1 - s]
            for s in (0, 1)
        ]

    tok, right = pl.pallas_call(
        functools.partial(token_kernel, root),
        in_specs=[ANY] * 6,
        out_specs=[VMEM] * 2,
        out_shape=[
            jax.ShapeDtypeStruct((width + META_ROWS, tokens), BF16),
            jax.ShapeDtypeStruct(root.shape, BF16),
        ],
        scratch_shapes=[
            pltpu.VMEM((topk, tokens), BF16),
            pltpu.VMEM((topk, tokens), jnp.int32),
            pltpu.VMEM((topk, tokens), jnp.int32),
            pltpu.VMEM((block, wide), BF16),
            pltpu.VMEM((rest, narrow), BF16),
            pltpu.VMEM((META_ROWS, tokens), F32),
            pltpu.SemaphoreType.DMA((6,)),
        ],
        compiler_params=params(56),
        cost_estimate=cost(),
        name="tokens",
    )(cotangent.T, gates.T, routes.T, slots.T, right_wide[0], right_narrow[0])

    def collect(values):
        count = len(values)
        return pl.pallas_call(
            functools.partial(collect_kernel, count),
            in_specs=[ANY] * count,
            out_specs=ANY,
            out_shape=jax.ShapeDtypeStruct((count,) + tok.shape, BF16),
            scratch_shapes=[pltpu.SemaphoreType.DMA((count,))],
            compiler_params=params(16),
            cost_estimate=cost(),
            name="collect",
        )(*values)

    def pack_left(wide_piece, narrow_piece):
        return pl.pallas_call(
            functools.partial(pack_left_kernel, left_root),
            in_specs=[ANY] * 2,
            out_shape=jax.ShapeDtypeStruct(left_root.shape, BF16),
            scratch_shapes=[
                pltpu.VMEM((block, wide), BF16),
                pltpu.VMEM((rest, narrow), BF16),
                pltpu.SemaphoreType.DMA((2,)),
            ],
            compiler_params=params(16),
            cost_estimate=cost(),
            name="pack_left",
        )(wide_piece, narrow_piece)

    chunk_rows = ffn // ROW_CHUNKS
    hidden = jnp.swapaxes(saved_hidden[0, 0], 1, 2)

    def partial(first, later, mine, theirs_first, theirs_later):
        return pl.pallas_call(
            functools.partial(partial_kernel, topk, width, block, gap, first, later),
            grid=(ROW_CHUNKS,),
            in_specs=[pl.BlockSpec((sources, chunk_rows, capacity), lambda i: (0, i, 0))]
            + [VMEM] * (1 + len(mine) + len(later)),
            out_specs=pl.BlockSpec((chunk_rows, span), lambda i: (i, 0)),
            out_shape=jax.ShapeDtypeStruct((ffn, span), BF16),
            scratch_shapes=[pltpu.VMEM((sources * capacity, span), BF16)],
            compiler_params=params(32),
            cost_estimate=cost(),
            name="partial",
        )(hidden, *mine, theirs_first, *theirs_later)

    def product(chain, t, value, got):
        keys = [(0, 0)]
        if t:
            keys = sorted({(chain.distance(t, z, s), s) for z in range(n) for s in (0, 1)})
            keys = [key for key in keys if key[0]]
        sets = chain.sets(t) if t else [0]
        made = pl.pallas_call(
            functools.partial(product_kernel, chain, t, keys, root, block, gap),
            in_specs=[VMEM] * (1 + len(keys)),
            out_specs=[VMEM] * len(sets),
            out_shape=[jax.ShapeDtypeStruct(chain.fold.shape, BF16)] * len(sets),
            scratch_shapes=[pltpu.VMEM(root.shape, BF16)],
            compiler_params=params(16),
            cost_estimate=cost(),
            name="product",
        )(value, *[got[far][s] for far, s in keys])
        return dict(zip(sets, made))

    def add(chain, t, s, term, got):
        return pl.pallas_call(
            functools.partial(add_kernel, chain, t, s),
            in_specs=[VMEM] * 2,
            out_specs=VMEM,
            out_shape=jax.ShapeDtypeStruct(term.shape, BF16),
            compiler_params=params(16),
            cost_estimate=cost(),
            name="add",
        )(term, got)

    order = Order(slots)
    straight = [m for m in range(1, chips) if m & (m - 1) == 0]
    mine = {0: tok}
    for m in straight:
        mine[m] = lax.ppermute(tok, "expert", [(i, i ^ (2 * m)) for i in range(experts)])
    got = [[right, right]]
    got.append(hop(1, got[0]))
    left = pack_left(left_wide[0], left_narrow[0])
    mine, got, left = order.gate((), (mine, got, left))

    first = [0] + straight
    later = [m for m in range(1, chips) if m not in straight]
    for m in later:
        mine[m] = lax.ppermute(mine[0], "expert", [(i, i ^ (2 * m)) for i in range(experts)])
    for k in range(2, n - 1):
        got.append(hop(k, got[-1]))

    def sibling(piece):
        return lax.ppermute(piece, "expert", [(i, i ^ 1) for i in range(experts)])

    theirs_first = sibling(collect([mine[m] for m in first]))
    ends = [pair for pair in gather_pairs(1, 0) if pair in ((0, 1), (n - 1, n - 2))]
    others = [pair for pair in gather_pairs(1, 0) if pair not in ends]
    left_ends = lax.ppermute(left, "dp", ends)
    theirs_later = [sibling(mine[m]) for m in later]
    value = partial(first, later, [mine[m] for m in first + later], theirs_first, theirs_later)
    got, left, left_ends, value = order.gate((), (got, left, left_ends, value))

    one, two = chains
    sent, terms = {}, {}

    def hop_one(pairs, piece):
        return lax.ppermute(piece, "dp", pairs) if pairs else piece

    def make(chain, t):
        terms[chain.half, t] = product(chain, t, value, got)

    def wait(keys, more=(), values=()):
        ready, _, values = order.gate((), ([sent[key] for key in keys], more, values))
        sent.update(zip(keys, ready))
        return values

    def go(chain, t, s):
        term = terms[chain.half, t][s]
        if chain.adds(t, s):
            term = add(chain, t, s, term, sent[chain.half, t - 1, 1 - s])
        sent[chain.half, t, s] = lax.ppermute(term, "dp", chain.pairs(t, s))

    make(one, 1)
    for s in one.sets(1):
        go(one, 1, s)
    for k in range(max(2, n - 1), n):
        got.append(hop(k, got[-1]))
    left_odd = hop_one(gather_pairs(1, 1), left)
    left_rest = hop_one(others, left)
    inner = {target for _, target in ends}
    if all(pair[0] in inner for pair in gather_pairs(2, 1)):
        left_even = left_ends
    else:
        z = lax.axis_index("dp")
        left_even = jnp.where((z == 1) | (z == n - 2), left_ends, left_rest)
    second = [None, hop_one(gather_pairs(2, 1), left_even)]
    own = [product(chain, 0, value, got)[0] for chain in chains]

    got, value, left_odd = wait([(0, 1, s) for s in one.sets(1)], (), (got, value, left_odd))
    make(two, 1)
    make(one, 2)
    for s in two.sets(1):
        go(two, 1, s)
    if n == 4:
        go(one, 2, 1)
        second[0] = hop_one(gather_pairs(2, 0), left_odd)
        left_rest, second[1], terms[0, 2] = wait([], (), (left_rest, second[1], terms[0, 2]))
        go(one, 2, 0)
        third = hop_one(gather_pairs(3, 0), second[1])
        make(two, 2)
        second[0], terms[1, 2] = wait([(1, 1, 0)], (), (second[0], terms[1, 2]))
        go(two, 2, 1)
        go(two, 2, 0)
        make(one, 3)
        terms[0, 3] = wait([(0, 2, 0), (0, 2, 1)], (), terms[0, 3])
        go(one, 3, 1)
        go(one, 3, 0)
        make(two, 3)
        third, terms[1, 3] = wait([(1, 2, 1)], (), (third, terms[1, 3]))
        go(two, 3, 0)
        make(one, 4)
        terms[1, 3] = wait([(1, 2, 0)], (), terms[1, 3])
        go(two, 3, 1)
        terms[0, 4] = wait([(0, 3, 1)], (), terms[0, 4])
        go(one, 4, 0)
        lefts = [[left, left], [left_even, left_odd], second, [third, third]]
    else:
        for s in one.sets(2):
            go(one, 2, s)
        second[0] = hop_one(gather_pairs(2, 0), left_odd)
        lefts = [[left, left], [left_even, left_odd], second]
        for t in range(2, max(chain.steps for chain in chains) + 1):
            for chain in chains:
                if t <= chain.steps and (chain.half, t) != (0, 2):
                    make(chain, t)
                    before = [(chain.half, t - 1, s) for s in chain.sets(t - 1)]
                    terms[chain.half, t] = wait(before, (), terms[chain.half, t])
                    for s in chain.sets(t):
                        go(chain, t, s)
            if 2 < t < n:
                lefts.append(hop(t, wait([], (), lefts[-1])))

    left_inputs = [left, left_ends, left_rest, left_odd] + [item for pair in lefts[2:] for item in pair]
    if n == 4:
        left_inputs = wait([(0, 3, 0)], (), left_inputs)
    left_w, left_n = pl.pallas_call(
        functools.partial(left_kernel, left_root, n),
        in_specs=[ANY] * len(left_inputs),
        out_shape=(
            jax.ShapeDtypeStruct((block, block), BF16),
            jax.ShapeDtypeStruct((rest, rest), BF16),
        ),
        scratch_shapes=[pltpu.VMEM((n,) + left_root.shape, BF16), pltpu.SemaphoreType.DMA((n,))],
        compiler_params=params(32),
        cost_estimate=cost(3),
        name="left",
    )(*left_inputs)

    keys = sorted({(chain.half, t, s) for chain in chains for here in range(n) for t, s in chain.arrivals(here)})
    last = [(0, one.steps, s) for s in one.sets(one.steps)] + [(1, two.steps, 1)]
    early = [key for key in keys if key not in last]
    last = [key for key in keys if key in last]
    own = wait(early, (left_w, left_n), own)
    totals = pl.pallas_call(
        functools.partial(total_kernel, chains, early),
        in_specs=[ANY] + [VMEM] * (len(chains) + len(early)),
        out_specs=[VMEM] * len(chains),
        out_shape=[jax.ShapeDtypeStruct(chain.fold.shape, F32) for chain in chains],
        compiler_params=params(32),
        cost_estimate=cost(3),
        name="total",
    )(order.tick, *own, *[sent[key] for key in early])
    out_w, out_n = pl.pallas_call(
        functools.partial(final_kernel, chains, block, last),
        in_specs=[VMEM] * (len(chains) + len(last) + 2),
        out_specs=[VMEM] * 2,
        out_shape=[jax.ShapeDtypeStruct((ffn, wide), F32), jax.ShapeDtypeStruct((ffn, narrow), F32)],
        scratch_shapes=[pltpu.VMEM(chain.fold.shape, BF16) for chain in chains]
        + [pltpu.VMEM((ffn, narrow), BF16)],
        compiler_params=params(32),
        cost_estimate=cost(),
        name="final",
    )(*totals, *[sent[key] for key in last], left_w, left_n)
    return out_w[None], out_n[None]


def solution(mesh):
    return jax.shard_map(
        body,
        mesh=mesh,
        in_specs=(
            P(("dp", "expert"), None),
            P(("dp", "expert"), None),
            P(("dp", "expert"), None),
            P(("dp", "expert"), None),
            P("dp", "expert", None, None, None),
            P("expert", None, "dp"),
            P("expert", None, "dp"),
            P("expert", None, "dp"),
            P("expert", None, "dp"),
        ),
        out_specs=(P("expert", None, "dp"), P("expert", None, "dp")),
        check_vma=False,
    )
```

```python
import functools

import jax
import jax.numpy as jnp
from jax import lax
from jax.experimental import pallas as pl
from jax.experimental.pallas import tpu as pltpu
from jax.sharding import PartitionSpec as P

BF16 = jnp.bfloat16
F32 = jnp.float32
LANES = 128
META_ROWS = 16
ROW_CHUNKS = 3
MIB = 1024 * 1024


def round_up(value, unit):
    return (value + unit - 1) // unit * unit


def params(mib):
    return pltpu.CompilerParams(vmem_limit_bytes=mib * MIB)


def cost(micros=0):
    return pl.CostEstimate(flops=int(micros * 1.15e9), bytes_accessed=0, transcendentals=0)


class Order:
    def __init__(self, tick):
        self.tick = tick

    def gate(self, ready, values):
        self.tick, _, values = lax.optimization_barrier((self.tick, ready, values))
        return values


def dot_nn(left, right):
    return lax.dot_general(left, right, (((1,), (0,)), ((), ())), preferred_element_type=F32)


def dot_nt(left, right):
    return lax.dot_general(left, right, (((1,), (1,)), ((), ())), preferred_element_type=F32)


ANY = pl.BlockSpec(memory_space=pl.ANY)
VMEM = pl.BlockSpec(memory_space=pltpu.VMEM)


class Fold:
    def __init__(self, rows_w, rows_n, wide, narrow, tuck=False):
        self.rows_w, self.rows_n, self.wide, self.narrow = rows_w, rows_n, wide, narrow
        self.lanes = round_up(wide, LANES)
        self.step = round_up(narrow, LANES)
        self.ways = max(1, self.lanes // self.step)
        while rows_n % (self.ways * 16):
            self.ways -= 1
        self.tucked, self.group = 0, narrow
        if tuck:
            for rows in range(16, min(rows_w, rows_n) + 1, 16):
                group = -(-narrow // (rows_w // rows))
                if group <= self.lanes - wide and (rows_n - rows) % (self.ways * 16) == 0:
                    self.tucked, self.group = rows, group
        self.part = (rows_n - self.tucked) // self.ways
        self.rows = rows_w + self.part
        self.shape = (self.rows, self.lanes)

    def places(self):
        found = []
        if self.tucked:
            for i, start in enumerate(range(0, self.narrow, self.group)):
                stop = min(self.narrow, start + self.group)
                found.append(
                    (
                        slice(0, self.tucked),
                        slice(start, stop),
                        slice(i * self.tucked, (i + 1) * self.tucked),
                        slice(self.wide, self.wide + stop - start),
                    )
                )
        for way in range(self.ways if self.part else 0):
            low = self.tucked + way * self.part
            found.append(
                (
                    slice(low, low + self.part),
                    slice(0, self.narrow),
                    slice(self.rows_w, self.rows),
                    slice(way * self.step, way * self.step + self.narrow),
                )
            )
        return found

    def write(self, ref, wide_value, narrow_value):
        ref[...] = jnp.zeros(self.shape, ref.dtype)
        ref[0 : self.rows_w, 0 : self.wide] = wide_value
        for rows, columns, at_rows, at_lanes in self.places():
            ref[at_rows, at_lanes] = narrow_value[rows, columns]

    def wide_of(self, value):
        return value[0 : self.rows_w, 0 : self.wide]

    def narrow_of(self, value):
        parts = [value[at_rows, at_lanes] for _, _, at_rows, at_lanes in self.places()]
        return parts[0] if len(parts) == 1 else jnp.concatenate(parts, axis=0)

    def put_narrow(self, value, ref, low_row, low_column):
        for rows, columns, at_rows, at_lanes in self.places():
            ref[
                low_row + rows.start : low_row + rows.stop, low_column + columns.start : low_column + columns.stop
            ] = value[at_rows, at_lanes]


def token_kernel(root, cot_ref, gate_ref, route_ref, slot_ref, rw_ref, rn_ref, tok_ref, right_ref,
                 gate, route, slot, wide, narrow, meta, sem):
    width = cot_ref.shape[0]
    ways = gate_ref.shape[0]
    sources = (rw_ref, rn_ref, gate_ref, route_ref, slot_ref, cot_ref)
    targets = (wide, narrow, gate, route, slot, tok_ref.at[pl.ds(0, width)])
    copies = [
        pltpu.make_async_copy(source, target, sem.at[i])
        for i, (source, target) in enumerate(zip(sources, targets))
    ]
    for copy in copies:
        copy.start()
    for copy in copies[:5]:
        copy.wait()
    root.write(right_ref, wide[...], narrow[...])
    meta[...] = jnp.zeros(meta.shape, F32)
    meta[0:ways, :] = gate[...].astype(F32)
    meta[ways : 2 * ways, :] = route[...].astype(F32)
    meta[2 * ways : 3 * ways, :] = slot[...].astype(F32)
    tok_ref[width : width + META_ROWS, :] = meta[...].astype(BF16)
    copies[5].wait()


def pack_left_kernel(root, lw_ref, ln_ref, out_ref, wide, narrow, sem):
    copies = [
        pltpu.make_async_copy(lw_ref, wide, sem.at[0]),
        pltpu.make_async_copy(ln_ref, narrow, sem.at[1]),
    ]
    for copy in copies:
        copy.start()
    for copy in copies:
        copy.wait()
    root.write(out_ref, wide[...], narrow[...])


def partial_kernel(topk, width, block, gap, first, later, hidden_ref, *refs):
    sources, _, capacity = hidden_ref.shape
    out_ref, rows_ref = refs[-2:]
    token_refs = {}
    for i, m in enumerate(first + later):
        token_refs[2 * m] = refs[i]
        if i < len(first):
            token_refs[2 * m + 1] = refs[len(first + later)].at[i]
        else:
            token_refs[2 * m + 1] = refs[len(first + later) + 1 + i - len(first)]
    expert = lax.axis_index("expert")
    parts = ((0, block, 0), (block, width, gap))

    @pl.when(pl.program_id(0) == 0)
    def _():
        for offset in range(sources):
            token_ref = token_refs[offset]
            source = jnp.bitwise_xor(expert, offset)
            meta = token_ref[width : width + META_ROWS, :].astype(F32)
            tokens = meta.shape[1]
            place = lax.broadcasted_iota(jnp.int32, (capacity, tokens), 0).astype(F32)
            here = expert.astype(F32)
            weights = jnp.zeros((capacity, tokens), F32)
            for k in range(topk):
                gate = meta[k : k + 1, :]
                route = meta[topk + k : topk + k + 1, :]
                slot = meta[2 * topk + k : 2 * topk + k + 1, :]
                wanted = jnp.where(route == here, slot, -1.0)
                weights = jnp.where(place == wanted, gate, weights)
            weights = weights.astype(BF16)
            rows = pl.ds(pl.multiple_of(source * capacity, capacity), capacity)
            for low, high, at in parts:
                value = dot_nt(weights, token_ref[low:high, :]).astype(BF16)
                rows_ref[rows, at : at + high - low] = value

    if capacity % LANES == 0:
        hidden = jnp.concatenate([hidden_ref[s] for s in range(sources)], axis=1)
    for low, high, at in parts:
        columns = slice(at, at + high - low)
        if capacity % LANES == 0:
            total = dot_nn(hidden, rows_ref[:, columns])
        else:
            total = dot_nn(hidden_ref[0], rows_ref[0:capacity, columns])
            for s in range(1, sources):
                total += dot_nn(hidden_ref[s], rows_ref[s * capacity : (s + 1) * capacity, columns])
        out_ref[:, columns] = total.astype(BF16)


class Chain:
    def __init__(self, n, half, order, low, fold):
        self.n, self.half, self.order, self.low, self.fold = n, half, order, low, fold
        self.steps = max(t for t in range(1, 2 * n) if self.pairs(t, 0) or self.pairs(t, 1))

    def distance(self, t, z, s):
        i = z if z % 2 == s else self.n - 1 - z
        if (z % 2 == s and z == self.n - 1) or (z % 2 != s and z == 0):
            return 0
        k = t - 1 - i
        if 0 <= k < len(self.order) and self.order[k] > i:
            return self.order[k] - i
        return 0

    def pairs(self, t, s):
        return [
            (z, z + 1 if z % 2 == s else z - 1) for z in range(self.n) if self.distance(t, z, s)
        ]

    def sets(self, t):
        return [s for s in (0, 1) if self.pairs(t, s)]

    def adds(self, t, s):
        targets = {target for _, target in self.pairs(t - 1, 1 - s)} if t > 1 else set()
        return any(z in targets for z, _ in self.pairs(t, s))

    def arrivals(self, z):
        found = []
        for t in range(1, self.steps + 1):
            for s in (0, 1):
                for sender, target in self.pairs(t, s):
                    if target == z and self.distance(t, sender, s) == 1:
                        found.append((t, s))
        return found


def product_kernel(chain, t, sets, keys, root, block, gap, partial_ref, *refs):
    root_refs = dict(zip(keys, refs))
    out_refs, piece_ref = refs[len(keys) : -1], refs[-1]
    z = lax.axis_index("dp")
    fold = chain.fold

    def product(root_ref, out_ref):
        piece = root_ref[...]
        rows = slice(chain.low, chain.low + fold.rows_w)
        wide = dot_nn(partial_ref[rows, 0:block], root.wide_of(piece))
        narrow = dot_nn(partial_ref[rows, gap : gap + root.rows_n], root.narrow_of(piece))
        fold.write(out_ref, wide.astype(BF16), narrow.astype(BF16))

    def take(root_ref):
        piece_ref[...] = root_ref[...]

    if t == 0:
        product(root_refs[0, 0], out_refs[0])
        return
    for s, out_ref in zip(sets, out_refs):
        by_far = {}
        for here in range(chain.n):
            far = chain.distance(t, here, s)
            if far:
                by_far[far] = by_far.get(far, False) | (z == here)
        if len(by_far) <= 2:
            for far, here in by_far.items():
                pl.when(here)(functools.partial(product, root_refs[far, s], out_ref))
        else:
            for far, here in by_far.items():
                pl.when(here)(functools.partial(take, root_refs[far, s]))
            here = functools.reduce(jnp.logical_or, by_far.values())
            pl.when(here)(functools.partial(product, piece_ref, out_ref))


def add_kernel(chain, t, s, term_ref, got_ref, out_ref):
    z = lax.axis_index("dp")
    sends = functools.reduce(jnp.logical_or, [z == here for here, _ in chain.pairs(t, s)])

    @pl.when(sends)
    def _():
        out_ref[...] = (term_ref[...].astype(F32) + got_ref[...].astype(F32)).astype(BF16)


def left_kernel(root, n, own_ref, ends_ref, rest_ref, odd_ref, *refs):
    got = refs[: 2 * (n - 2)]
    wide_ref, narrow_ref, held, sem = refs[2 * (n - 2) :]
    z = lax.axis_index("dp")
    for here in range(n):
        even_ref = ends_ref if here in (1, n - 2) else rest_ref
        near = (even_ref, odd_ref) + got

        @pl.when(z == here)
        def _():
            copies = [pltpu.make_async_copy(own_ref, held.at[here], sem.at[here])]
            for q in range(n):
                if q != here:
                    s = here % 2 if q > here else 1 - here % 2
                    copies.append(
                        pltpu.make_async_copy(near[2 * (abs(q - here) - 1) + s], held.at[q], sem.at[q])
                    )
            for copy in copies:
                copy.start()
            for copy in copies:
                copy.wait()

    for q in range(n):
        piece = held[q]
        wide_ref[:, q * root.wide : (q + 1) * root.wide] = root.wide_of(piece)
        root.put_narrow(piece, narrow_ref, 0, q * root.narrow)


def add_arrivals(chains, got_refs, own_refs, out_refs, dtype):
    z = lax.axis_index("dp")
    for here in range(chains[0].n):

        @pl.when(z == here)
        def _():
            for chain, own_ref, out_ref in zip(chains, own_refs, out_refs):
                value = own_ref[...].astype(F32)
                for t, s in chain.arrivals(here):
                    if (chain.half, t, s) in got_refs:
                        value += got_refs[chain.half, t, s][...].astype(F32)
                out_ref[...] = value.astype(dtype)


def total_kernel(chains, keys, order_ref, *refs):
    got_refs = dict(zip(keys, refs[len(chains) :]))
    add_arrivals(chains, got_refs, refs[: len(chains)], refs[len(chains) + len(keys) :], F32)


def final_kernel(chains, block, keys, *refs):
    got_refs = dict(zip(keys, refs[len(chains) :]))
    wide_ref, narrow_ref, out_w_ref, out_n_ref = refs[len(chains) + len(keys) :][:4]
    totals, narrow_rows = refs[len(refs) - len(chains) - 1 : -1], refs[-1]
    add_arrivals(chains, got_refs, refs[: len(chains)], totals, BF16)
    values = [total[...] for total in totals]
    for chain, value in zip(chains, values):
        chain.fold.put_narrow(value, narrow_rows, chain.low, 0)
    wide_rows = jnp.concatenate([chain.fold.wide_of(value) for chain, value in zip(chains, values)], axis=0)
    for rows, out_ref in ((wide_rows, out_w_ref), (narrow_rows[...], out_n_ref)):
        out_ref[0:block, :] = dot_nn(wide_ref[...], rows[0:block])
        out_ref[block:, :] = dot_nn(narrow_ref[...], rows[block:])


def collect_kernel(count, *refs):
    sem = refs[-1]
    out_ref = refs[count]
    copies = [pltpu.make_async_copy(refs[i], out_ref.at[i], sem.at[i]) for i in range(count)]
    for copy in copies:
        copy.start()
    for copy in copies:
        copy.wait()


def body(
    cotangent, gates, routes, slots, saved_hidden, left_wide, left_narrow, right_wide, right_narrow
):
    tokens, width = cotangent.shape
    topk = gates.shape[1]
    n = lax.axis_size("dp")
    experts = lax.axis_size("expert")
    chips = experts // 2
    _, _, sources, capacity, ffn = saved_hidden.shape
    block, wide = right_wide.shape[1:]
    rest, narrow = right_narrow.shape[1:]
    gap = round_up(block, LANES)
    span = gap + round_up(rest, LANES)
    root = Fold(block, rest, wide, narrow)
    left_root = Fold(block, rest, wide, narrow, True)
    cut = ffn // 64 * 32
    folds = [Fold(rows, rows, wide, narrow, True) for rows in (cut, ffn - cut)]
    sooner = [n - 2, n - 1] if n > 2 else [1]
    chains = [
        Chain(n, 0, sooner + list(range(n - 3, 0, -1)), 0, folds[0]),
        Chain(n, 1, list(range(n - 1, 0, -1)), cut, folds[1]),
    ]

    def gather_pairs(k, s):
        up = [(i, i + 1) for i in range(s, n - 1, 2) if i >= k - 1]
        return up + [(i + 1, i) for i in range(s, n - 1, 2) if i <= n - 1 - k]

    def hop(k, pieces):
        return [
            lax.ppermute(pieces[1 - s], "dp", gather_pairs(k, s)) if gather_pairs(k, s) else pieces[1 - s]
            for s in (0, 1)
        ]

    tok, right = pl.pallas_call(
        functools.partial(token_kernel, root),
        in_specs=[ANY] * 6,
        out_specs=[VMEM] * 2,
        out_shape=[
            jax.ShapeDtypeStruct((width + META_ROWS, tokens), BF16),
            jax.ShapeDtypeStruct(root.shape, BF16),
        ],
        scratch_shapes=[
            pltpu.VMEM((topk, tokens), BF16),
            pltpu.VMEM((topk, tokens), jnp.int32),
            pltpu.VMEM((topk, tokens), jnp.int32),
            pltpu.VMEM((block, wide), BF16),
            pltpu.VMEM((rest, narrow), BF16),
            pltpu.VMEM((META_ROWS, tokens), F32),
            pltpu.SemaphoreType.DMA((6,)),
        ],
        compiler_params=params(56),
        cost_estimate=cost(),
        name="tokens",
    )(cotangent.T, gates.T, routes.T, slots.T, right_wide[0], right_narrow[0])

    def collect(values):
        count = len(values)
        return pl.pallas_call(
            functools.partial(collect_kernel, count),
            in_specs=[ANY] * count,
            out_specs=ANY,
            out_shape=jax.ShapeDtypeStruct((count,) + tok.shape, BF16),
            scratch_shapes=[pltpu.SemaphoreType.DMA((count,))],
            compiler_params=params(16),
            cost_estimate=cost(),
            name="collect",
        )(*values)

    def pack_left(wide_piece, narrow_piece):
        return pl.pallas_call(
            functools.partial(pack_left_kernel, left_root),
            in_specs=[ANY] * 2,
            out_shape=jax.ShapeDtypeStruct(left_root.shape, BF16),
            scratch_shapes=[
                pltpu.VMEM((block, wide), BF16),
                pltpu.VMEM((rest, narrow), BF16),
                pltpu.SemaphoreType.DMA((2,)),
            ],
            compiler_params=params(16),
            cost_estimate=cost(),
            name="pack_left",
        )(wide_piece, narrow_piece)

    chunk_rows = ffn // ROW_CHUNKS
    hidden = jnp.swapaxes(saved_hidden[0, 0], 1, 2)

    def partial(first, later, mine, theirs_first, theirs_later):
        return pl.pallas_call(
            functools.partial(partial_kernel, topk, width, block, gap, first, later),
            grid=(ROW_CHUNKS,),
            in_specs=[pl.BlockSpec((sources, chunk_rows, capacity), lambda i: (0, i, 0))]
            + [VMEM] * (1 + len(mine) + len(later)),
            out_specs=pl.BlockSpec((chunk_rows, span), lambda i: (i, 0)),
            out_shape=jax.ShapeDtypeStruct((ffn, span), BF16),
            scratch_shapes=[pltpu.VMEM((sources * capacity, span), BF16)],
            compiler_params=params(32),
            cost_estimate=cost(),
            name="partial",
        )(hidden, *mine, theirs_first, *theirs_later)

    def product(chain, t, value, got, sets=None, micros=0):
        sets = sets or (chain.sets(t) if t else [0])
        keys = [(0, 0)]
        if t:
            keys = sorted({(chain.distance(t, z, s), s) for z in range(n) for s in sets})
            keys = [key for key in keys if key[0]]
        made = pl.pallas_call(
            functools.partial(product_kernel, chain, t, sets, keys, root, block, gap),
            in_specs=[VMEM] * (1 + len(keys)),
            out_specs=[VMEM] * len(sets),
            out_shape=[jax.ShapeDtypeStruct(chain.fold.shape, BF16)] * len(sets),
            scratch_shapes=[pltpu.VMEM(root.shape, BF16)],
            compiler_params=params(16),
            cost_estimate=cost(micros),
            name="product",
        )(value, *[got[far][s] for far, s in keys])
        return dict(zip(sets, made))

    def add(chain, t, s, term, got):
        return pl.pallas_call(
            functools.partial(add_kernel, chain, t, s),
            in_specs=[VMEM] * 2,
            out_specs=VMEM,
            out_shape=jax.ShapeDtypeStruct(term.shape, BF16),
            compiler_params=params(16),
            cost_estimate=cost(),
            name="add",
        )(term, got)

    order = Order(slots.T)
    straight = [m for m in range(1, chips) if m & (m - 1) == 0]
    mine = {0: tok}
    for m in straight:
        mine[m] = lax.ppermute(tok, "expert", [(i, i ^ (2 * m)) for i in range(experts)])
    got = [[right, right]]
    got.append(hop(1, got[0]))
    left = pack_left(left_wide[0], left_narrow[0])
    mine, got, left = order.gate((), (mine, got, left))

    first = [0] + straight
    later = [m for m in range(1, chips) if m not in straight]
    for m in later:
        mine[m] = lax.ppermute(mine[0], "expert", [(i, i ^ (2 * m)) for i in range(experts)])
    for k in range(2, n - 1):
        got.append(hop(k, got[-1]))

    def sibling(piece):
        return lax.ppermute(piece, "expert", [(i, i ^ 1) for i in range(experts)])

    theirs_first = sibling(collect([mine[m] for m in first]))
    ends = [pair for pair in gather_pairs(1, 0) if pair in ((0, 1), (n - 1, n - 2))]
    others = [pair for pair in gather_pairs(1, 0) if pair not in ends]
    left_ends = lax.ppermute(left, "dp", ends)
    theirs_later = [sibling(mine[m]) for m in later]
    value = partial(first, later, [mine[m] for m in first + later], theirs_first, theirs_later)
    got, left, value = order.gate((), (got, left, value))

    one, two = chains
    sent, terms = {}, {}

    def hop_one(pairs, piece):
        return lax.ppermute(piece, "dp", pairs) if pairs else piece

    def make(chain, t, sets=None, micros=0):
        terms.setdefault((chain.half, t), {}).update(product(chain, t, value, got, sets, micros))

    def wait(keys, more=(), values=()):
        ready, _, values = order.gate((), ([sent[key] for key in keys], more, values))
        sent.update(zip(keys, ready))
        return values

    def go(chain, t, s):
        term = terms[chain.half, t][s]
        if chain.adds(t, s):
            term = add(chain, t, s, term, sent[chain.half, t - 1, 1 - s])
        sent[chain.half, t, s] = lax.ppermute(term, "dp", chain.pairs(t, s))

    make(one, 1)
    for s in one.sets(1):
        go(one, 1, s)
    for k in range(max(2, n - 1), n):
        got.append(hop(k, got[-1]))
    left_odd = hop_one(gather_pairs(1, 1), left)
    left_rest = hop_one(others, left)
    left_ends, value = wait([], (), (left_ends, value))
    inner = {target for _, target in ends}
    if all(pair[0] in inner for pair in gather_pairs(2, 1)):
        left_even = left_ends
    else:
        z = lax.axis_index("dp")
        left_even = jnp.where((z == 1) | (z == n - 2), left_ends, left_rest)
    second = [None, hop_one(gather_pairs(2, 1), left_even)]
    own = [product(chain, 0, value, got)[0] for chain in chains]

    if n == 4:
        make(one, 2, [1], 4)
        got, value, terms[0, 2] = wait([(0, 1, 0)], (), (got, value, terms[0, 2]))
    else:
        got, value, left_odd = wait([(0, 1, s) for s in one.sets(1)], (), (got, value, left_odd))
        make(one, 2)
    make(two, 1)
    for s in two.sets(1):
        go(two, 1, s)
    if n == 4:
        go(one, 2, 1)
        make(one, 2, [0])
        left_rest, left_odd, terms[0, 2] = wait([], (), (left_rest, left_odd, terms[0, 2]))
        go(one, 2, 0)
        second[0] = hop_one(gather_pairs(2, 0), left_odd)
        make(two, 2)
        terms[1, 2] = wait([(1, 1, 0)], (), terms[1, 2])
        go(two, 2, 1)
        second[1] = wait([], (), second[1])
        third = hop_one(gather_pairs(3, 0), second[1])
        second[0], terms[1, 2] = wait([], (), (second[0], terms[1, 2]))
        go(two, 2, 0)
        make(one, 3)
        terms[0, 3] = wait([(0, 2, 0), (0, 2, 1)], (), terms[0, 3])
        go(one, 3, 1)
        go(one, 3, 0)
        make(two, 3)
        third, terms[1, 3] = wait([(1, 2, 1)], (), (third, terms[1, 3]))
        go(two, 3, 0)
        make(one, 4)
        terms[1, 3] = wait([(1, 2, 0)], (), terms[1, 3])
        go(two, 3, 1)
        terms[0, 4] = wait([(0, 3, 1)], (), terms[0, 4])
        go(one, 4, 0)
        lefts = [[left, left], [left_even, left_odd], second, [third, third]]
    else:
        for s in one.sets(2):
            go(one, 2, s)
        second[0] = hop_one(gather_pairs(2, 0), left_odd)
        lefts = [[left, left], [left_even, left_odd], second]
        for t in range(2, max(chain.steps for chain in chains) + 1):
            for chain in chains:
                if t <= chain.steps and (chain.half, t) != (0, 2):
                    make(chain, t)
                    before = [(chain.half, t - 1, s) for s in chain.sets(t - 1)]
                    terms[chain.half, t] = wait(before, (), terms[chain.half, t])
                    for s in chain.sets(t):
                        go(chain, t, s)
            if 2 < t < n:
                lefts.append(hop(t, wait([], (), lefts[-1])))

    left_inputs = [left, left_ends, left_rest, left_odd] + [item for pair in lefts[2:] for item in pair]
    left_w, left_n = pl.pallas_call(
        functools.partial(left_kernel, left_root, n),
        in_specs=[ANY] * len(left_inputs),
        out_shape=(
            jax.ShapeDtypeStruct((block, block), BF16),
            jax.ShapeDtypeStruct((rest, rest), BF16),
        ),
        scratch_shapes=[pltpu.VMEM((n,) + left_root.shape, BF16), pltpu.SemaphoreType.DMA((n,))],
        compiler_params=params(32),
        cost_estimate=cost(),
        name="left",
    )(*left_inputs)

    keys = sorted({(chain.half, t, s) for chain in chains for here in range(n) for t, s in chain.arrivals(here)})
    last = [(0, one.steps, s) for s in one.sets(one.steps)] + [(1, two.steps, 1)]
    early = [key for key in keys if key not in last]
    last = [key for key in keys if key in last]
    own = wait(early, (left_w, left_n), own)
    totals = pl.pallas_call(
        functools.partial(total_kernel, chains, early),
        in_specs=[ANY] + [VMEM] * (len(chains) + len(early)),
        out_specs=[VMEM] * len(chains),
        out_shape=[jax.ShapeDtypeStruct(chain.fold.shape, F32) for chain in chains],
        compiler_params=params(32),
        cost_estimate=cost(3),
        name="total",
    )(order.tick, *own, *[sent[key] for key in early])
    out_w, out_n = pl.pallas_call(
        functools.partial(final_kernel, chains, block, last),
        in_specs=[VMEM] * (len(chains) + len(last) + 2),
        out_specs=[VMEM] * 2,
        out_shape=[jax.ShapeDtypeStruct((ffn, wide), F32), jax.ShapeDtypeStruct((ffn, narrow), F32)],
        scratch_shapes=[pltpu.VMEM(chain.fold.shape, BF16) for chain in chains]
        + [pltpu.VMEM((ffn, narrow), BF16)],
        compiler_params=params(32),
        cost_estimate=cost(),
        name="final",
    )(*totals, *[sent[key] for key in last], left_w, left_n)
    return out_w[None], out_n[None]


def solution(mesh):
    return jax.shard_map(
        body,
        mesh=mesh,
        in_specs=(
            P(("dp", "expert"), None),
            P(("dp", "expert"), None),
            P(("dp", "expert"), None),
            P(("dp", "expert"), None),
            P("dp", "expert", None, None, None),
            P("expert", None, "dp"),
            P("expert", None, "dp"),
            P("expert", None, "dp"),
            P("expert", None, "dp"),
        ),
        out_specs=(P("expert", None, "dp"), P("expert", None, "dp")),
        check_vma=False,
    )
```

```python
import functools

import jax
import jax.numpy as jnp
from jax import lax
from jax.experimental import pallas as pl
from jax.experimental.pallas import tpu as pltpu
from jax.sharding import PartitionSpec as P

BF16 = jnp.bfloat16
F32 = jnp.float32
LANES = 128
META_ROWS = 16
ROW_CHUNKS = 3
MIB = 1024 * 1024


def round_up(value, unit):
    return (value + unit - 1) // unit * unit


def params(mib):
    return pltpu.CompilerParams(vmem_limit_bytes=mib * MIB)


def cost(micros=0):
    return pl.CostEstimate(flops=int(micros * 1.15e9), bytes_accessed=0, transcendentals=0)


class Order:
    def __init__(self, tick):
        self.tick = tick

    def gate(self, ready, values):
        self.tick, _, values = lax.optimization_barrier((self.tick, ready, values))
        return values


def dot_nn(left, right):
    return lax.dot_general(left, right, (((1,), (0,)), ((), ())), preferred_element_type=F32)


def dot_nt(left, right):
    return lax.dot_general(left, right, (((1,), (1,)), ((), ())), preferred_element_type=F32)


ANY = pl.BlockSpec(memory_space=pl.ANY)
VMEM = pl.BlockSpec(memory_space=pltpu.VMEM)


class Fold:
    def __init__(self, rows_w, rows_n, wide, narrow, tuck=False):
        self.rows_w, self.rows_n, self.wide, self.narrow = rows_w, rows_n, wide, narrow
        self.lanes = round_up(wide, LANES)
        self.step = round_up(narrow, LANES)
        self.ways = max(1, self.lanes // self.step)
        while rows_n % (self.ways * 16):
            self.ways -= 1
        self.tucked, self.group = 0, narrow
        if tuck:
            for rows in range(16, min(rows_w, rows_n) + 1, 16):
                group = -(-narrow // (rows_w // rows))
                if group <= self.lanes - wide and (rows_n - rows) % (self.ways * 16) == 0:
                    self.tucked, self.group = rows, group
        self.part = (rows_n - self.tucked) // self.ways
        self.rows = rows_w + self.part
        self.shape = (self.rows, self.lanes)

    def places(self):
        found = []
        if self.tucked:
            for i, start in enumerate(range(0, self.narrow, self.group)):
                stop = min(self.narrow, start + self.group)
                found.append(
                    (
                        slice(0, self.tucked),
                        slice(start, stop),
                        slice(i * self.tucked, (i + 1) * self.tucked),
                        slice(self.wide, self.wide + stop - start),
                    )
                )
        for way in range(self.ways if self.part else 0):
            low = self.tucked + way * self.part
            found.append(
                (
                    slice(low, low + self.part),
                    slice(0, self.narrow),
                    slice(self.rows_w, self.rows),
                    slice(way * self.step, way * self.step + self.narrow),
                )
            )
        return found

    def write(self, ref, wide_value, narrow_value):
        ref[...] = jnp.zeros(self.shape, ref.dtype)
        ref[0 : self.rows_w, 0 : self.wide] = wide_value
        for rows, columns, at_rows, at_lanes in self.places():
            ref[at_rows, at_lanes] = narrow_value[rows, columns]

    def wide_of(self, value):
        return value[0 : self.rows_w, 0 : self.wide]

    def narrow_of(self, value):
        parts = [value[at_rows, at_lanes] for _, _, at_rows, at_lanes in self.places()]
        return parts[0] if len(parts) == 1 else jnp.concatenate(parts, axis=0)

    def put_narrow(self, value, ref, low_row, low_column):
        for rows, columns, at_rows, at_lanes in self.places():
            ref[
                low_row + rows.start : low_row + rows.stop, low_column + columns.start : low_column + columns.stop
            ] = value[at_rows, at_lanes]


def token_kernel(root, cot_ref, gate_ref, route_ref, slot_ref, rw_ref, rn_ref, tok_ref, right_ref,
                 gate, route, slot, wide, narrow, meta, sem):
    width = cot_ref.shape[0]
    ways = gate_ref.shape[0]
    sources = (rw_ref, rn_ref, gate_ref, route_ref, slot_ref, cot_ref)
    targets = (wide, narrow, gate, route, slot, tok_ref.at[pl.ds(0, width)])
    copies = [
        pltpu.make_async_copy(source, target, sem.at[i])
        for i, (source, target) in enumerate(zip(sources, targets))
    ]
    for copy in copies:
        copy.start()
    for copy in copies[:5]:
        copy.wait()
    root.write(right_ref, wide[...], narrow[...])
    meta[...] = jnp.zeros(meta.shape, F32)
    meta[0:ways, :] = gate[...].astype(F32)
    meta[ways : 2 * ways, :] = route[...].astype(F32)
    meta[2 * ways : 3 * ways, :] = slot[...].astype(F32)
    tok_ref[width : width + META_ROWS, :] = meta[...].astype(BF16)
    copies[5].wait()


def pack_left_kernel(root, lw_ref, ln_ref, out_ref, wide, narrow, sem):
    copies = [
        pltpu.make_async_copy(lw_ref, wide, sem.at[0]),
        pltpu.make_async_copy(ln_ref, narrow, sem.at[1]),
    ]
    for copy in copies:
        copy.start()
    for copy in copies:
        copy.wait()
    root.write(out_ref, wide[...], narrow[...])


def partial_kernel(topk, width, block, gap, first, later, hidden_ref, *refs):
    sources, _, capacity = hidden_ref.shape
    out_ref, rows_ref = refs[-2:]
    token_refs = {}
    for i, m in enumerate(first + later):
        token_refs[2 * m] = refs[i]
        if i < len(first):
            token_refs[2 * m + 1] = refs[len(first + later)].at[i]
        else:
            token_refs[2 * m + 1] = refs[len(first + later) + 1 + i - len(first)]
    expert = lax.axis_index("expert")
    parts = ((0, block, 0), (block, width, gap))

    @pl.when(pl.program_id(0) == 0)
    def _():
        for offset in range(sources):
            token_ref = token_refs[offset]
            source = jnp.bitwise_xor(expert, offset)
            meta = token_ref[width : width + META_ROWS, :].astype(F32)
            tokens = meta.shape[1]
            place = lax.broadcasted_iota(jnp.int32, (capacity, tokens), 0).astype(F32)
            here = expert.astype(F32)
            weights = jnp.zeros((capacity, tokens), F32)
            for k in range(topk):
                gate = meta[k : k + 1, :]
                route = meta[topk + k : topk + k + 1, :]
                slot = meta[2 * topk + k : 2 * topk + k + 1, :]
                wanted = jnp.where(route == here, slot, -1.0)
                weights = jnp.where(place == wanted, gate, weights)
            weights = weights.astype(BF16)
            rows = pl.ds(pl.multiple_of(source * capacity, capacity), capacity)
            for low, high, at in parts:
                value = dot_nt(weights, token_ref[low:high, :]).astype(BF16)
                rows_ref[rows, at : at + high - low] = value

    if capacity % LANES == 0:
        hidden = jnp.concatenate([hidden_ref[s] for s in range(sources)], axis=1)
    for low, high, at in parts:
        columns = slice(at, at + high - low)
        if capacity % LANES == 0:
            total = dot_nn(hidden, rows_ref[:, columns])
        else:
            total = dot_nn(hidden_ref[0], rows_ref[0:capacity, columns])
            for s in range(1, sources):
                total += dot_nn(hidden_ref[s], rows_ref[s * capacity : (s + 1) * capacity, columns])
        out_ref[:, columns] = total.astype(BF16)


class Chain:
    def __init__(self, n, half, order, low, fold):
        self.n, self.half, self.order, self.low, self.fold = n, half, order, low, fold
        self.steps = max(t for t in range(1, 2 * n) if self.pairs(t, 0) or self.pairs(t, 1))

    def distance(self, t, z, s):
        i = z if z % 2 == s else self.n - 1 - z
        if (z % 2 == s and z == self.n - 1) or (z % 2 != s and z == 0):
            return 0
        k = t - 1 - i
        if 0 <= k < len(self.order) and self.order[k] > i:
            return self.order[k] - i
        return 0

    def pairs(self, t, s):
        return [
            (z, z + 1 if z % 2 == s else z - 1) for z in range(self.n) if self.distance(t, z, s)
        ]

    def sets(self, t):
        return [s for s in (0, 1) if self.pairs(t, s)]

    def adds(self, t, s):
        targets = {target for _, target in self.pairs(t - 1, 1 - s)} if t > 1 else set()
        return any(z in targets for z, _ in self.pairs(t, s))

    def arrivals(self, z):
        found = []
        for t in range(1, self.steps + 1):
            for s in (0, 1):
                for sender, target in self.pairs(t, s):
                    if target == z and self.distance(t, sender, s) == 1:
                        found.append((t, s))
        return found


def product_kernel(chain, t, sets, keys, root, block, gap, partial_ref, *refs):
    root_refs = dict(zip(keys, refs))
    out_refs, piece_ref = refs[len(keys) : -1], refs[-1]
    z = lax.axis_index("dp")
    fold = chain.fold

    def product(root_ref, out_ref):
        piece = root_ref[...]
        rows = slice(chain.low, chain.low + fold.rows_w)
        wide = dot_nn(partial_ref[rows, 0:block], root.wide_of(piece))
        narrow = dot_nn(partial_ref[rows, gap : gap + root.rows_n], root.narrow_of(piece))
        fold.write(out_ref, wide.astype(BF16), narrow.astype(BF16))

    def take(root_ref):
        piece_ref[...] = root_ref[...]

    if t == 0:
        product(root_refs[0, 0], out_refs[0])
        return
    for s, out_ref in zip(sets, out_refs):
        by_far = {}
        for here in range(chain.n):
            far = chain.distance(t, here, s)
            if far:
                by_far[far] = by_far.get(far, False) | (z == here)
        if len(by_far) <= 2:
            for far, here in by_far.items():
                pl.when(here)(functools.partial(product, root_refs[far, s], out_ref))
        else:
            for far, here in by_far.items():
                pl.when(here)(functools.partial(take, root_refs[far, s]))
            here = functools.reduce(jnp.logical_or, by_far.values())
            pl.when(here)(functools.partial(product, piece_ref, out_ref))


def add_kernel(chain, t, s, term_ref, got_ref, out_ref):
    z = lax.axis_index("dp")
    sends = functools.reduce(jnp.logical_or, [z == here for here, _ in chain.pairs(t, s)])

    @pl.when(sends)
    def _():
        out_ref[...] = (term_ref[...].astype(F32) + got_ref[...].astype(F32)).astype(BF16)


def left_kernel(root, n, own_ref, ends_ref, rest_ref, odd_ref, *refs):
    got = refs[: 2 * (n - 2)]
    wide_ref, narrow_ref, held, sem = refs[2 * (n - 2) :]
    z = lax.axis_index("dp")
    for here in range(n):
        even_ref = ends_ref if here in (1, n - 2) else rest_ref
        near = (even_ref, odd_ref) + got

        @pl.when(z == here)
        def _():
            copies = [pltpu.make_async_copy(own_ref, held.at[here], sem.at[here])]
            for q in range(n):
                if q != here:
                    s = here % 2 if q > here else 1 - here % 2
                    copies.append(
                        pltpu.make_async_copy(near[2 * (abs(q - here) - 1) + s], held.at[q], sem.at[q])
                    )
            for copy in copies:
                copy.start()
            for copy in copies:
                copy.wait()

    for q in range(n):
        piece = held[q]
        wide_ref[:, q * root.wide : (q + 1) * root.wide] = root.wide_of(piece)
        root.put_narrow(piece, narrow_ref, 0, q * root.narrow)


def add_arrivals(chains, got_refs, own_refs, out_refs, dtype):
    z = lax.axis_index("dp")
    for here in range(chains[0].n):

        @pl.when(z == here)
        def _():
            for chain, own_ref, out_ref in zip(chains, own_refs, out_refs):
                value = own_ref[...].astype(F32)
                for t, s in chain.arrivals(here):
                    if (chain.half, t, s) in got_refs:
                        value += got_refs[chain.half, t, s][...].astype(F32)
                out_ref[...] = value.astype(dtype)


def total_kernel(chains, keys, order_ref, *refs):
    got_refs = dict(zip(keys, refs[len(chains) :]))
    add_arrivals(chains, got_refs, refs[: len(chains)], refs[len(chains) + len(keys) :], F32)


def final_kernel(chains, block, keys, *refs):
    got_refs = dict(zip(keys, refs[len(chains) :]))
    wide_ref, narrow_ref, out_w_ref, out_n_ref = refs[len(chains) + len(keys) :][:4]
    totals, narrow_rows = refs[len(refs) - len(chains) - 1 : -1], refs[-1]
    add_arrivals(chains, got_refs, refs[: len(chains)], totals, BF16)
    values = [total[...] for total in totals]
    for chain, value in zip(chains, values):
        chain.fold.put_narrow(value, narrow_rows, chain.low, 0)
    wide_rows = jnp.concatenate([chain.fold.wide_of(value) for chain, value in zip(chains, values)], axis=0)
    for rows, out_ref in ((wide_rows, out_w_ref), (narrow_rows[...], out_n_ref)):
        out_ref[0:block, :] = dot_nn(wide_ref[...], rows[0:block])
        out_ref[block:, :] = dot_nn(narrow_ref[...], rows[block:])


def collect_kernel(count, *refs):
    sem = refs[-1]
    out_ref = refs[count]
    copies = [pltpu.make_async_copy(refs[i], out_ref.at[i], sem.at[i]) for i in range(count)]
    for copy in copies:
        copy.start()
    for copy in copies:
        copy.wait()


def body(
    cotangent, gates, routes, slots, saved_hidden, left_wide, left_narrow, right_wide, right_narrow
):
    tokens, width = cotangent.shape
    topk = gates.shape[1]
    n = lax.axis_size("dp")
    experts = lax.axis_size("expert")
    chips = experts // 2
    _, _, sources, capacity, ffn = saved_hidden.shape
    block, wide = right_wide.shape[1:]
    rest, narrow = right_narrow.shape[1:]
    gap = round_up(block, LANES)
    span = gap + round_up(rest, LANES)
    root = Fold(block, rest, wide, narrow)
    left_root = Fold(block, rest, wide, narrow, True)
    cut = ffn // 64 * 32
    folds = [Fold(rows, rows, wide, narrow, True) for rows in (cut, ffn - cut)]
    sooner = [n - 2, n - 1] if n > 2 else [1]
    chains = [
        Chain(n, 0, sooner + list(range(n - 3, 0, -1)), 0, folds[0]),
        Chain(n, 1, list(range(n - 1, 0, -1)), cut, folds[1]),
    ]

    def gather_pairs(k, s):
        up = [(i, i + 1) for i in range(s, n - 1, 2) if i >= k - 1]
        return up + [(i + 1, i) for i in range(s, n - 1, 2) if i <= n - 1 - k]

    def hop(k, pieces):
        return [
            lax.ppermute(pieces[1 - s], "dp", gather_pairs(k, s)) if gather_pairs(k, s) else pieces[1 - s]
            for s in (0, 1)
        ]

    tok, right = pl.pallas_call(
        functools.partial(token_kernel, root),
        in_specs=[ANY] * 6,
        out_specs=[VMEM] * 2,
        out_shape=[
            jax.ShapeDtypeStruct((width + META_ROWS, tokens), BF16),
            jax.ShapeDtypeStruct(root.shape, BF16),
        ],
        scratch_shapes=[
            pltpu.VMEM((topk, tokens), BF16),
            pltpu.VMEM((topk, tokens), jnp.int32),
            pltpu.VMEM((topk, tokens), jnp.int32),
            pltpu.VMEM((block, wide), BF16),
            pltpu.VMEM((rest, narrow), BF16),
            pltpu.VMEM((META_ROWS, tokens), F32),
            pltpu.SemaphoreType.DMA((6,)),
        ],
        compiler_params=params(56),
        cost_estimate=cost(),
        name="tokens",
    )(cotangent.T, gates.T, routes.T, slots.T, right_wide[0], right_narrow[0])

    def collect(values):
        count = len(values)
        return pl.pallas_call(
            functools.partial(collect_kernel, count),
            in_specs=[ANY] * count,
            out_specs=ANY,
            out_shape=jax.ShapeDtypeStruct((count,) + tok.shape, BF16),
            scratch_shapes=[pltpu.SemaphoreType.DMA((count,))],
            compiler_params=params(16),
            cost_estimate=cost(),
            name="collect",
        )(*values)

    def pack_left(wide_piece, narrow_piece):
        return pl.pallas_call(
            functools.partial(pack_left_kernel, left_root),
            in_specs=[ANY] * 2,
            out_shape=jax.ShapeDtypeStruct(left_root.shape, BF16),
            scratch_shapes=[
                pltpu.VMEM((block, wide), BF16),
                pltpu.VMEM((rest, narrow), BF16),
                pltpu.SemaphoreType.DMA((2,)),
            ],
            compiler_params=params(16),
            cost_estimate=cost(),
            name="pack_left",
        )(wide_piece, narrow_piece)

    chunk_rows = ffn // ROW_CHUNKS
    hidden = jnp.swapaxes(saved_hidden[0, 0], 1, 2)

    def partial(first, later, mine, theirs_first, theirs_later):
        return pl.pallas_call(
            functools.partial(partial_kernel, topk, width, block, gap, first, later),
            grid=(ROW_CHUNKS,),
            in_specs=[pl.BlockSpec((sources, chunk_rows, capacity), lambda i: (0, i, 0))]
            + [VMEM] * (1 + len(mine) + len(later)),
            out_specs=pl.BlockSpec((chunk_rows, span), lambda i: (i, 0)),
            out_shape=jax.ShapeDtypeStruct((ffn, span), BF16),
            scratch_shapes=[pltpu.VMEM((sources * capacity, span), BF16)],
            compiler_params=params(32),
            cost_estimate=cost(),
            name="partial",
        )(hidden, *mine, theirs_first, *theirs_later)

    def product(chain, t, value, got, sets=None, micros=0):
        sets = sets or (chain.sets(t) if t else [0])
        keys = [(0, 0)]
        if t:
            keys = sorted({(chain.distance(t, z, s), s) for z in range(n) for s in sets})
            keys = [key for key in keys if key[0]]
        made = pl.pallas_call(
            functools.partial(product_kernel, chain, t, sets, keys, root, block, gap),
            in_specs=[VMEM] * (1 + len(keys)),
            out_specs=[VMEM] * len(sets),
            out_shape=[jax.ShapeDtypeStruct(chain.fold.shape, BF16)] * len(sets),
            scratch_shapes=[pltpu.VMEM(root.shape, BF16)],
            compiler_params=params(16),
            cost_estimate=cost(micros),
            name="product",
        )(value, *[got[far][s] for far, s in keys])
        return dict(zip(sets, made))

    def add(chain, t, s, term, got):
        return pl.pallas_call(
            functools.partial(add_kernel, chain, t, s),
            in_specs=[VMEM] * 2,
            out_specs=VMEM,
            out_shape=jax.ShapeDtypeStruct(term.shape, BF16),
            compiler_params=params(16),
            cost_estimate=cost(),
            name="add",
        )(term, got)

    order = Order(slots.T)
    straight = [m for m in range(1, chips) if m & (m - 1) == 0]
    mine = {0: tok}
    for m in straight:
        mine[m] = lax.ppermute(tok, "expert", [(i, i ^ (2 * m)) for i in range(experts)])
    got = [[right, right]]
    got.append(hop(1, got[0]))
    left = pack_left(left_wide[0], left_narrow[0])
    mine, got, left = order.gate((), (mine, got, left))

    first = [0] + straight
    later = [m for m in range(1, chips) if m not in straight]
    for m in later:
        mine[m] = lax.ppermute(mine[0], "expert", [(i, i ^ (2 * m)) for i in range(experts)])
    for k in range(2, n - 1):
        got.append(hop(k, got[-1]))

    def sibling(piece):
        return lax.ppermute(piece, "expert", [(i, i ^ 1) for i in range(experts)])

    theirs_first = sibling(collect([mine[m] for m in first]))
    ends = [pair for pair in gather_pairs(1, 0) if pair in ((0, 1), (n - 1, n - 2))]
    others = [pair for pair in gather_pairs(1, 0) if pair not in ends]
    left_ends = lax.ppermute(left, "dp", ends)
    theirs_later = [sibling(mine[m]) for m in later]
    value = partial(first, later, [mine[m] for m in first + later], theirs_first, theirs_later)
    got, left, value = order.gate((), (got, left, value))

    one, two = chains
    sent, terms = {}, {}

    def hop_one(pairs, piece):
        return lax.ppermute(piece, "dp", pairs) if pairs else piece

    def make(chain, t, sets=None, micros=0):
        terms.setdefault((chain.half, t), {}).update(product(chain, t, value, got, sets, micros))

    def wait(keys, more=(), values=()):
        ready, _, values = order.gate((), ([sent[key] for key in keys], more, values))
        sent.update(zip(keys, ready))
        return values

    def go(chain, t, s):
        term = terms[chain.half, t][s]
        if chain.adds(t, s):
            term = add(chain, t, s, term, sent[chain.half, t - 1, 1 - s])
        sent[chain.half, t, s] = lax.ppermute(term, "dp", chain.pairs(t, s))

    make(one, 1)
    for s in one.sets(1):
        go(one, 1, s)
    for k in range(max(2, n - 1), n):
        got.append(hop(k, got[-1]))
    left_odd = hop_one(gather_pairs(1, 1), left)
    left_rest = hop_one(others, left)
    left_ends, value = wait([], (), (left_ends, value))
    inner = {target for _, target in ends}
    if all(pair[0] in inner for pair in gather_pairs(2, 1)):
        left_even = left_ends
    else:
        z = lax.axis_index("dp")
        left_even = jnp.where((z == 1) | (z == n - 2), left_ends, left_rest)
    second = [None, hop_one(gather_pairs(2, 1), left_even)]
    own = [product(chain, 0, value, got)[0] for chain in chains]

    if n == 4:
        make(one, 2, [1], 4)
        got, value, terms[0, 2] = wait([(0, 1, 0)], (), (got, value, terms[0, 2]))
    else:
        got, value, left_odd = wait([(0, 1, s) for s in one.sets(1)], (), (got, value, left_odd))
        make(one, 2)
    make(two, 1)
    for s in two.sets(1):
        go(two, 1, s)
    if n == 4:
        go(one, 2, 1)
        make(one, 2, [0])
        left_rest, left_odd, terms[0, 2] = wait([], (), (left_rest, left_odd, terms[0, 2]))
        go(one, 2, 0)
        second[0] = hop_one(gather_pairs(2, 0), left_odd)
        make(two, 2)
        terms[1, 2] = wait([(1, 1, 0)], (), terms[1, 2])
        go(two, 2, 1)
        second[1] = wait([], (), second[1])
        third = hop_one(gather_pairs(3, 0), second[1])
        go(two, 2, 0)
        make(one, 3)
        terms[0, 3], value = wait([(0, 2, 1)], (), (terms[0, 3], value))
        make(one, 4, None, 1)
        second[0], terms[0, 3], terms[0, 4] = wait([(0, 2, 0)], (), (second[0], terms[0, 3], terms[0, 4]))
        go(one, 3, 1)
        go(one, 3, 0)
        make(two, 3)
        third, terms[1, 3] = wait([(1, 2, 1)], (), (third, terms[1, 3]))
        go(two, 3, 0)
        terms[1, 3] = wait([(1, 2, 0)], (), terms[1, 3])
        go(two, 3, 1)
        terms[0, 4] = wait([(0, 3, 1)], (), terms[0, 4])
        go(one, 4, 0)
        lefts = [[left, left], [left_even, left_odd], second, [third, third]]
    else:
        for s in one.sets(2):
            go(one, 2, s)
        second[0] = hop_one(gather_pairs(2, 0), left_odd)
        lefts = [[left, left], [left_even, left_odd], second]
        for t in range(2, max(chain.steps for chain in chains) + 1):
            for chain in chains:
                if t <= chain.steps and (chain.half, t) != (0, 2):
                    make(chain, t)
                    before = [(chain.half, t - 1, s) for s in chain.sets(t - 1)]
                    terms[chain.half, t] = wait(before, (), terms[chain.half, t])
                    for s in chain.sets(t):
                        go(chain, t, s)
            if 2 < t < n:
                lefts.append(hop(t, wait([], (), lefts[-1])))

    left_inputs = [left, left_ends, left_rest, left_odd] + [item for pair in lefts[2:] for item in pair]
    left_w, left_n = pl.pallas_call(
        functools.partial(left_kernel, left_root, n),
        in_specs=[ANY] * len(left_inputs),
        out_shape=(
            jax.ShapeDtypeStruct((block, block), BF16),
            jax.ShapeDtypeStruct((rest, rest), BF16),
        ),
        scratch_shapes=[pltpu.VMEM((n,) + left_root.shape, BF16), pltpu.SemaphoreType.DMA((n,))],
        compiler_params=params(32),
        cost_estimate=cost(),
        name="left",
    )(*left_inputs)

    keys = sorted({(chain.half, t, s) for chain in chains for here in range(n) for t, s in chain.arrivals(here)})
    last = [(0, one.steps, s) for s in one.sets(one.steps)] + [(1, two.steps, 1)]
    early = [key for key in keys if key not in last]
    last = [key for key in keys if key in last]
    own = wait(early, (left_w, left_n), own)
    totals = pl.pallas_call(
        functools.partial(total_kernel, chains, early),
        in_specs=[ANY] + [VMEM] * (len(chains) + len(early)),
        out_specs=[VMEM] * len(chains),
        out_shape=[jax.ShapeDtypeStruct(chain.fold.shape, F32) for chain in chains],
        compiler_params=params(32),
        cost_estimate=cost(3),
        name="total",
    )(order.tick, *own, *[sent[key] for key in early])
    out_w, out_n = pl.pallas_call(
        functools.partial(final_kernel, chains, block, last),
        in_specs=[VMEM] * (len(chains) + len(last) + 2),
        out_specs=[VMEM] * 2,
        out_shape=[jax.ShapeDtypeStruct((ffn, wide), F32), jax.ShapeDtypeStruct((ffn, narrow), F32)],
        scratch_shapes=[pltpu.VMEM(chain.fold.shape, BF16) for chain in chains]
        + [pltpu.VMEM((ffn, narrow), BF16)],
        compiler_params=params(32),
        cost_estimate=cost(),
        name="final",
    )(*totals, *[sent[key] for key in last], left_w, left_n)
    return out_w[None], out_n[None]


def solution(mesh):
    return jax.shard_map(
        body,
        mesh=mesh,
        in_specs=(
            P(("dp", "expert"), None),
            P(("dp", "expert"), None),
            P(("dp", "expert"), None),
            P(("dp", "expert"), None),
            P("dp", "expert", None, None, None),
            P("expert", None, "dp"),
            P("expert", None, "dp"),
            P("expert", None, "dp"),
            P("expert", None, "dp"),
        ),
        out_specs=(P("expert", None, "dp"), P("expert", None, "dp")),
        check_vma=False,
    )
```
